256 devices in a mesh: occ: 64 (over z, x, y_hi), vir: 4 (over y_lo, core).
Axes of the slice: x: 4, y: 4 (y_hi: 2, y_lo: 2; y = y_hi * 2 + y_lo), z: 8, core: 2. Of those that a mesh axis runs over, the one named last changes fastest.
Arguments:
- amplitudes: bfloat16 [64, 384, 64, 384], P('occ', 'vir'), may hold values from -6 to 6
- aux_ints: bfloat16 [384, 64, 1024], P('vir', None, 'occ'), may hold values from -0.109375 to 0.109375
- occ_irrep: int32 [64], replicated, may hold values from 0 to 7, as said below
- vir_irrep: int32 [384], replicated, may hold values from 0 to 7, as said below
Outputs:
- residual: bfloat16 [64, 384, 64, 384], P('occ', 'vir')
The draws below stay inside these ranges and needn't reach their ends.
Inputs may be any that keep to these rules, and one draw needn't show every extreme that they name: `occ_irrep`: labels of the eight D2h irreps (a product of orbitals is totally symmetric when the XOR of their labels is 0); orbitals are ordered by irrep, labels never fall, and each irrep holds a multiple of 8 orbitals, possibly none. `vir_irrep`: labels of the eight D2h irreps; orbitals are ordered by irrep, labels never fall, and each irrep holds a multiple of 24 orbitals, possibly none.
All inputs are finite; a program needn't handle non-finite values.
Results may differ from the reference program's by a relative error of at most 0.0066.
Values may be sent and summed in bfloat16 or wider, within the bound.
A program may use at most 128 MiB of HBM per device.

```python
import jax
import jax.numpy as jnp
from jax import lax

O = 64
V = 384
NAUX = 1024


def sorted_runs(key, units, run_length):
    middle = jax.random.randint(key, (units - 2,), 0, 8, dtype=jnp.int32)
    ends = jnp.array([0, 7], dtype=jnp.int32)
    labels = jnp.sort(jnp.concatenate([ends, middle]))
    return jnp.repeat(labels, run_length, total_repeat_length=units * run_length)


def draw_occ_irrep(key, part):
    key = jax.random.fold_in(key, 11)
    return sorted_runs(key, 8, O // 8)


def draw_vir_irrep(key, part):
    key = jax.random.fold_in(key, 23)
    return sorted_runs(key, 16, V // 16)


def level_of(rng, extent, pieces, low, top_value):
    level, own = 1.0, jax.random.fold_in(rng, 6)
    for axis_at, shards_of in pieces:
        steps = jnp.exp(jax.random.uniform(jax.random.fold_in(own, axis_at), (shards_of,), jnp.float32, low / len(pieces), top_value / len(pieces)))
        level = level * jnp.repeat(steps, extent[axis_at] // shards_of).reshape([-1 if axis == axis_at else 1 for axis in range(len(extent))])
    return level


def centred(rng, shape, spread, reach, split=(), kind=jnp.bfloat16):
    values = jax.random.normal(rng, shape, jnp.float32) * spread
    if len(split) > 0:
        values = level_of(rng, shape, split, -0.22, 0.18) * values
    return jnp.clip(values, min=-reach, max=reach).astype(kind)


def setup_inputs(seed: int = 0) -> dict:
    arg_keys = jax.random.split(jax.random.key(seed), 5)
    amplitudes = centred(arg_keys[0], (O, V, O, V), 1.0, 6.0, ((0, 64), (1, 4)))
    aux_ints = centred(arg_keys[1], (V, O, NAUX), (O * V // 8) ** -0.5, 0.109375, ((0, 4), (2, 64)))
    occ_irrep = draw_occ_irrep(jax.random.fold_in(arg_keys[4], 71), 0)
    vir_irrep = draw_vir_irrep(jax.random.fold_in(arg_keys[4], 71), 0)
    return dict(amplitudes=amplitudes, aux_ints=aux_ints, occ_irrep=occ_irrep, vir_irrep=vir_irrep)


def reference(amplitudes, aux_ints, occ_irrep, vir_irrep):
    aux_wide = aux_ints.astype(jnp.float32)

    def single_row(index):
        row_block = lax.dynamic_index_in_dim(amplitudes, index, 0, keepdims=False)
        row_label = lax.dynamic_index_in_dim(occ_irrep, index, 0, keepdims=False)
        labels = row_label ^ vir_irrep[:, None, None] ^ occ_irrep[None, :, None] ^ vir_irrep[None, None, :]
        masked = jnp.where(labels == 0, row_block, jnp.zeros_like(row_block))
        swapped = jnp.transpose(masked, (2, 1, 0))
        combined = (2.0 * masked.astype(jnp.float32) - swapped.astype(jnp.float32)).astype(jnp.bfloat16)
        partial_value = jnp.einsum('cka,ckp->ap', combined.astype(jnp.float32), aux_wide)
        fitted = partial_value.astype(jnp.bfloat16)
        cycle_row = jnp.einsum('bjp,ap->bja', aux_wide, fitted.astype(jnp.float32))
        return cycle_row.astype(jnp.bfloat16)

    cycle_term = lax.map(single_row, jnp.arange(O, dtype=jnp.int32))
    mirror = jnp.transpose(cycle_term, (2, 3, 0, 1))
    return (cycle_term.astype(jnp.float32) + mirror.astype(jnp.float32)).astype(jnp.bfloat16)
```

```python
import functools

import jax
import jax.numpy as jnp
from jax import lax
from jax.experimental import pallas as pl
from jax.experimental.pallas import tpu as pltpu
from jax.sharding import PartitionSpec as P

MESH = pl.DeviceIdType.MESH
NZ, NX, NY, NV = 8, 4, 2, 4
BF16, F32 = jnp.bfloat16, jnp.float32
GROUPS = ((0,), (1, 7), (2, 6), (3, 5), (4,))
COLUMNS = ((0,), (1, 3), (2,))
N_SEMS = 76


def position():
    o, v = lax.axis_index("occ"), lax.axis_index("vir")
    return o // (NX * NY), (o // NY) % NX, o % NY, v


def device(z, x, y, v):
    return ((z * NX + x) * NY + y, v)


def barrier(peers):
    sem = pltpu.get_barrier_semaphore()
    for peer in peers:
        pl.semaphore_signal(sem, 1, device_id=peer, device_id_type=MESH)
    pl.semaphore_wait(sem, len(peers))


def peers_of(z, x, y, v):
    ring = [
        device((z + 1) % NZ, x, y, v),
        device((z + NZ - 1) % NZ, x, y, v),
        device(z, (x + 1) % NX, y, v),
        device(z, (x + NX - 1) % NX, y, v),
        device(z, x, 1 - y, v),
    ]
    return ring + [device(z, x, y, (v + d) % NV) for d in range(1, NV)]


class Gather:
    def __init__(self, ref, rows, cut, send_sems, recv_sems):
        self.ref, self.rows, self.cut = ref, rows, cut
        self.width = ref.shape[1]
        self.send_sems, self.recv_sems = send_sems, recv_sems
        self.z, self.x, self.y, self.v = position()
        self.started = []

    def block(self, z, x, half):
        rows = self.rows
        if half is None:
            start, size = (z * NX + x) * NY * rows, NY * rows
        else:
            start, size = ((z * NX + x) * NY + half) * rows, rows
        return pl.ds(pl.multiple_of(start, 16), size)

    def copy(self, key, z, x, half, d):
        kind = key[0]
        index = {"az": 0, "ax": 8, "bx": 40, "bz": 44}[kind]
        if kind == "az":
            index += key[1] * 4 + key[2]
        elif kind == "ax":
            index += (key[1] * 8 + key[2]) * 2 + key[3]
        elif kind == "bx":
            index += key[1] * 2 + key[2]
        else:
            index += (key[1] * 4 + key[2]) * 4 + key[3]
        lanes = pl.ds(0, self.cut) if kind[0] == "a" else pl.ds(self.cut, self.width - self.cut)
        part = self.ref.at[self.block(z % NZ, x % NX, half), lanes]
        s = 1 - 2 * d
        if kind[1] == "z":
            target = device((self.z + s + NZ) % NZ, self.x, self.y, self.v)
        else:
            target = device(self.z, (self.x + s + NX) % NX, self.y, self.v)
        return pltpu.make_async_remote_copy(
            src_ref=part, dst_ref=part, send_sem=self.send_sems.at[index],
            recv_sem=self.recv_sems.at[index], device_id=target, device_id_type=MESH)

    def start(self, *args):
        copy = self.copy(*args)
        copy.start()
        self.started.append(args)

    def wait(self, *args):
        self.copy(*args).wait_recv()

    def az_send(self, d, t):
        s = 1 - 2 * d
        self.start(("az", d, t), self.z - s * t + NZ, self.x, d if t == 3 else None, d)

    def az_wait(self, d, t):
        s = 1 - 2 * d
        self.wait(("az", d, t), self.z - s * (t + 1) + NZ, self.x, d if t == 3 else None, d)

    def ax_send(self, d, delta, kind):
        s = 1 - 2 * d
        if kind == 0:
            self.start(("ax", d, delta, 0), self.z + delta, self.x, None, d)
        else:
            self.start(("ax", d, delta, 1), self.z + delta, self.x - s + NX, d, d)

    def ax_wait(self, d, delta, kind):
        s = 1 - 2 * d
        if kind == 0:
            self.wait(("ax", d, delta, 0), self.z + delta, self.x - s + NX, None, d)
        else:
            self.wait(("ax", d, delta, 1), self.z + delta, self.x - 2 * s + NX, d, d)

    def bx_send(self, d, kind):
        s = 1 - 2 * d
        if kind == 0:
            self.start(("bx", d, 0), self.z, self.x, None, d)
        else:
            self.start(("bx", d, 1), self.z, self.x - s + NX, d, d)

    def bx_wait(self, d, kind):
        s = 1 - 2 * d
        if kind == 0:
            self.wait(("bx", d, 0), self.z, self.x - s + NX, None, d)
        else:
            self.wait(("bx", d, 1), self.z, self.x - 2 * s + NX, d, d)

    def bz_send(self, d, xi, t):
        s = 1 - 2 * d
        self.start(("bz", d, xi, t), self.z - s * t + NZ, self.x + xi, d if t == 3 else None, d)

    def bz_wait(self, d, xi, t):
        s = 1 - 2 * d
        self.wait(("bz", d, xi, t), self.z - s * (t + 1) + NZ, self.x + xi, d if t == 3 else None, d)

    def wave(self, w):
        both = (0, 1)
        if w == 0:
            for d in both:
                self.az_send(d, 0)
                self.bx_send(d, 0)
            for d in both:
                self.ax_send(d, 0, 0)
                self.bz_send(d, 0, 0)
            return
        if w <= 4:
            for d in both:
                self.az_wait(d, w - 1)
                if w <= 3:
                    self.az_send(d, w)
            for delta in GROUPS[w]:
                for d in both:
                    self.ax_send(d, delta, 0)
        if w == 1:
            for d in both:
                self.bx_wait(d, 0)
                self.bx_send(d, 1)
            for xi in COLUMNS[1]:
                for d in both:
                    self.bz_send(d, xi, 0)
        if w == 2:
            for d in both:
                self.bx_wait(d, 1)
            for d in both:
                self.bz_send(d, 2, 0)
        if w <= 5:
            for delta in GROUPS[w - 1]:
                for d in both:
                    self.ax_wait(d, delta, 0)
                    self.ax_send(d, delta, 1)
        for u in range(3):
            t = w - 1 - u
            if 0 <= t <= 3:
                for xi in COLUMNS[u]:
                    for d in both:
                        self.bz_wait(d, xi, t)
                        if t <= 2:
                            self.bz_send(d, xi, t + 1)
        if w >= 2:
            for delta in GROUPS[w - 2]:
                for d in both:
                    self.ax_wait(d, delta, 1)

    def finish(self):
        for args in self.started:
            self.copy(*args).wait_send()


def fit_kernel(t_hbm, b_hbm, w_ref, vir_ref, bg_hbm, f_ref, bv_ref,
               t_v, tf0, tf1, tf2, cd, u, s, bg, accd, accs, fpart, fown, frecv, bvt,
               g_send, g_recv, t_send, t_recv, f_send, f_recv, one):
    z, x, y, v = position()
    o = (z * NX + x) * NY + y
    load_t = pltpu.make_async_copy(t_hbm, t_v, one.at[0])
    load_t.start()
    own = pl.ds(pl.multiple_of(o * 16, 16), 16)
    load_b = pltpu.make_async_copy(b_hbm, bg.at[own, :], one.at[1])
    load_b.start()
    barrier(peers_of(z, x, y, v))
    load_b.wait()
    swap = pltpu.make_async_remote_copy(
        src_ref=bg.at[own, :], dst_ref=bg.at[own, :], send_sem=one.at[2], recv_sem=one.at[3],
        device_id=device(z, x, 1 - y, v), device_id_type=MESH)
    swap.start()
    load_t.wait()

    labels = w_ref[...]

    def mask_row(c, _):
        row = t_v[c].astype(F32)
        row = jnp.where(labels == vir_ref[c], row, 0.0)
        for n, tf in enumerate((tf0, tf1, tf2)):
            tf[pl.ds(pl.multiple_of(c * 64, 64), 64), :] = row[:, 128 * n:128 * n + 128]
        return 0

    lax.fori_loop(0, 96, mask_row, 0)

    theirs = pl.ds(pl.multiple_of((o - y + 1 - y) * 16, 16), 16)
    pltpu.make_async_remote_copy(
        src_ref=bg.at[theirs, :], dst_ref=bg.at[theirs, :], send_sem=one.at[2], recv_sem=one.at[3],
        device_id=device(z, x, 1 - y, v), device_id_type=MESH).wait_recv()
    gather = Gather(bg, 16, 3712, g_send, g_recv)
    gather.wave(0)

    def turn(g, _):
        k = g * 4
        for n, tf in enumerate((tf0, tf1, tf2)):
            cols = pl.ds(128 * n, 128)
            rows = [tf[pl.ds(k + m, 96, stride=64), :] for m in range(4)]
            for m in range(4):
                cd[pl.ds(pl.multiple_of((k + m) * 96, 96), 96), cols] = rows[m].astype(BF16)
            for m in range(3):
                packed = jnp.concatenate([rows[m], rows[3][32 * m:32 * m + 32]], axis=0)
                u[g, m, cols, :] = packed.T.astype(BF16)
        return 0

    def t_copy(d, sb):
        to = (v + d) % NV
        return pltpu.make_async_remote_copy(
            src_ref=u.at[pl.ds(4 * sb, 4), :, pl.ds(pl.multiple_of(to * 96, 96), 96), :],
            dst_ref=s.at[pl.ds(4 * sb, 4), pl.ds(0, 3), :, pl.ds(pl.multiple_of(v * 128, 128), 128)],
            send_sem=t_send.at[d - 1, sb], recv_sem=t_recv.at[d - 1, sb],
            device_id=device(z, x, y, to), device_id_type=MESH)

    def t_wait(d, sb):
        frm = (v + NV - d) % NV
        pltpu.make_async_remote_copy(
            src_ref=u.at[pl.ds(4 * sb, 4), :, pl.ds(0, 96), :],
            dst_ref=s.at[pl.ds(4 * sb, 4), pl.ds(0, 3), :, pl.ds(pl.multiple_of(frm * 128, 128), 128)],
            send_sem=t_send.at[d - 1, sb], recv_sem=t_recv.at[d - 1, sb],
            device_id=device(z, x, y, frm), device_id_type=MESH).wait_recv()

    for sb in range(4):
        lax.fori_loop(4 * sb, 4 * sb + 4, turn, 0)
        for d in range(1, NV):
            t_copy(d, sb).start()
    mine = pltpu.make_async_copy(
        u.at[:, :, pl.ds(pl.multiple_of(v * 96, 96), 96), :],
        s.at[:, pl.ds(0, 3), :, pl.ds(pl.multiple_of(v * 128, 128), 128)], one.at[0])
    mine.start()

    pairs = ((0, 1), (7, 2), (6, 3), (5, 4))

    def zrow(delta):
        return pl.multiple_of(((z + delta) % NZ) * 128, 128)

    def times(pair, weights, acc):
        starts = [zrow(delta) for delta in pair]

        def step(kb, _):
            lanes = pl.ds(pl.multiple_of(kb * 768, 768), 768)
            left = jnp.concatenate([bg[pl.ds(a, 128), lanes] for a in starts], axis=0)
            part = jnp.dot(left, weights(kb), preferred_element_type=F32)
            for n, a in enumerate(starts):
                old = acc[pl.ds(a, 128), :]
                acc[pl.ds(a, 128), :] = jnp.where(kb == 0, 0.0, old) + part[128 * n:128 * n + 128]
            return 0

        lax.fori_loop(0, 8, step, 0)

    def out_copy(delta):
        rows = pl.ds(zrow(delta), 128)
        return pltpu.make_async_copy(bg.at[rows, :], bg_hbm.at[rows, :], one.at[4 + delta])

    def direct(n):
        times(pairs[n], lambda kb: cd[pl.ds(pl.multiple_of(kb * 768, 768), 768), :], accd)
        for delta in pairs[n]:
            out_copy(delta).start()

    def f_copy(d, delta, wait):
        lanes = pl.ds(zrow(delta), 128)
        other = (v + NV - d) % NV if wait else (v + d) % NV
        here = other if wait else v
        return pltpu.make_async_remote_copy(
            src_ref=fpart.at[other, :, lanes], dst_ref=frecv.at[here, :, lanes],
            send_sem=f_send.at[d - 1, delta], recv_sem=f_recv.at[d - 1, delta],
            device_id=device(z, x, y, other), device_id_type=MESH)

    def swapped(n):
        times(pairs[n], lambda kb: s[pl.ds(kb * 2, 2)].reshape(768, 512), accs)
        for delta in pairs[n]:
            rows = pl.ds(zrow(delta), 128)
            dt = accd[rows, :].T
            st = accs[rows, :].T
            for blk in range(NV):
                part = 2.0 * dt[96 * blk:96 * blk + 96] - st[128 * blk:128 * blk + 96]
                fpart[blk, :, rows] = part.astype(BF16)
                fown[blk, :, rows] = part
            for d in range(1, NV):
                f_copy(d, delta, False).start()

    gather.wave(1)
    gather.wave(2)
    gather.wave(3)
    direct(0)
    gather.wave(4)
    direct(1)
    gather.wave(5)
    direct(2)
    mine.wait()
    for sb in range(4):
        for d in range(1, NV):
            t_wait(d, sb)

    lane = lax.broadcasted_iota(jnp.int32, (96, 128), 1)

    def unpack(g, _):
        for blk in range(NV):
            lanes = pl.ds(128 * blk, 128)
            first = pltpu.roll(s[g, 0, :, lanes].astype(F32), 32, 1)
            second = pltpu.roll(s[g, 1, :, lanes].astype(F32), 64, 1)
            third = pltpu.roll(s[g, 2, :, lanes].astype(F32), 96, 1)
            s[g, 3, :, lanes] = jnp.where(lane < 32, first, jnp.where(lane < 64, second, third)).astype(BF16)
        return 0

    lax.fori_loop(0, 16, unpack, 0)
    for n in range(3):
        swapped(n)
    gather.wave(6)
    direct(3)
    swapped(3)

    four = bg[:, pl.ds(pl.multiple_of((o // 4) * 384, 384), 384)]
    bvt[...] = four.astype(F32).T.astype(BF16)
    bv_ref[...] = bvt[pl.ds(pl.multiple_of((o % 4) * 96, 96), 96), :]

    for d in range(1, NV):
        for delta in range(NZ):
            f_copy(d, delta, True).wait_recv()
    total = fown[v]
    for d in range(1, NV):
        total = total + frecv[(v + NV - d) % NV].astype(F32)
    f_ref[...] = total.astype(BF16)

    for d in range(1, NV):
        for delta in range(NZ):
            f_copy(d, delta, False).wait_send()
        for sb in range(4):
            t_copy(d, sb).wait_send()
    swap.wait_send()
    for delta in range(NZ):
        out_copy(delta).wait()
    gather.finish()


def cycle_kernel(bg_hbm, f_hbm, bv_hbm, r_ref,
                 bg, fg, wf, bvf, wft, bvt, g_send, g_recv, w_send, w_recv, one):
    z, x, y, v = position()
    o = (z * NX + x) * NY + y
    load = pltpu.make_async_copy(bg_hbm, bg, one.at[0])
    load.start()
    own = pl.ds(pl.multiple_of(o * 96, 96), 96)
    mine = pl.ds(pl.multiple_of(v * 96, 96), 96)
    loads = [
        pltpu.make_async_copy(f_hbm, fg.at[own, :], one.at[1]),
        pltpu.make_async_copy(f_hbm, wf.at[mine, :], one.at[2]),
        pltpu.make_async_copy(bv_hbm, bvf.at[mine, :], one.at[3]),
    ]
    for copy in loads:
        copy.start()
    barrier(peers_of(z, x, y, v))
    for copy in loads:
        copy.wait()

    def swap_copy(there):
        rows = pl.ds(pl.multiple_of((o - y + there) * 96, 96), 96)
        return pltpu.make_async_remote_copy(
            src_ref=fg.at[rows, :], dst_ref=fg.at[rows, :], send_sem=one.at[4], recv_sem=one.at[5],
            device_id=device(z, x, 1 - y, v), device_id_type=MESH)

    swap_copy(y).start()

    def w_copy(d, which, wait):
        ref = (wf, bvf)[which]
        other = (v + NV - d) % NV if wait else (v + d) % NV
        rows = pl.ds(pl.multiple_of((other if wait else v) * 96, 96), 96)
        return pltpu.make_async_remote_copy(
            src_ref=ref.at[rows, :], dst_ref=ref.at[rows, :], send_sem=w_send.at[which, d - 1],
            recv_sem=w_recv.at[which, d - 1], device_id=device(z, x, y, other), device_id_type=MESH)

    for which in range(2):
        for d in range(1, NV):
            w_copy(d, which, False).start()
    swap_copy(1 - y).wait_recv()
    gather = Gather(fg, 96, 640, g_send, g_recv)
    gather.wave(0)
    for d in range(1, NV):
        w_copy(d, 0, True).wait_recv()
    wft[...] = wf[...].astype(F32).T.astype(BF16)
    load.wait()

    def direct(n, _):
        lanes = pl.ds(pl.multiple_of(n * 384, 384), 384)
        part = lax.dot_general(bg[:, lanes], wft[...], (((0,), (0,)), ((), ())), preferred_element_type=F32)
        r_ref[pl.ds(pl.multiple_of(n * 384, 384), 384), :] = part.astype(BF16)
        return 0

    def mirror(delta):
        start = pl.multiple_of(((z + delta) % NZ) * 768, 768)

        def step(n, _):
            rows = pl.ds(pl.multiple_of(start + n * 384, 384), 384)
            part = jnp.dot(fg[rows, :], bvt[...], preferred_element_type=F32)
            r_ref[rows, :] = (r_ref[rows, :].astype(F32) + part).astype(BF16)
            return 0

        lax.fori_loop(0, 2, step, 0)

    lax.fori_loop(0, 4, direct, 0)
    gather.wave(1)
    lax.fori_loop(4, 8, direct, 0)
    gather.wave(2)
    lax.fori_loop(8, 12, direct, 0)
    gather.wave(3)
    lax.fori_loop(12, 16, direct, 0)
    for d in range(1, NV):
        w_copy(d, 1, True).wait_recv()
    bvt[...] = bvf[...].astype(F32).T.astype(BF16)
    gather.wave(4)
    for t in range(3):
        for delta in GROUPS[t]:
            mirror(delta)
    gather.wave(5)
    for delta in GROUPS[3]:
        mirror(delta)
    gather.wave(6)
    mirror(4)

    swap_copy(y).wait_send()
    for which in range(2):
        for d in range(1, NV):
            w_copy(d, which, False).wait_send()
    gather.finish()


def on_device(amplitudes, aux_ints, occ_irrep, vir_irrep):
    o, v = lax.axis_index("occ"), lax.axis_index("vir")
    labels = lax.dynamic_slice_in_dim(occ_irrep, o, 1)[:, None] ^ occ_irrep[:, None] ^ vir_irrep[None, :]
    block = lax.dynamic_slice_in_dim(vir_irrep, v * 96, 96)
    shard = jnp.transpose(aux_ints, (2, 1, 0)).reshape(16, 6144)
    any_spec = pl.BlockSpec(memory_space=pl.ANY)
    vmem_spec = pl.BlockSpec(memory_space=pltpu.VMEM)
    dma, vmem = pltpu.SemaphoreType.DMA, pltpu.VMEM
    bg, f, bv = pl.pallas_call(
        fit_kernel,
        name="fit",
        out_shape=(
            jax.ShapeDtypeStruct((1024, 6144), BF16),
            jax.ShapeDtypeStruct((96, 1024), BF16),
            jax.ShapeDtypeStruct((96, 1024), BF16),
        ),
        in_specs=[any_spec, any_spec, vmem_spec, pl.BlockSpec(memory_space=pltpu.SMEM)],
        out_specs=(any_spec, vmem_spec, vmem_spec),
        scratch_shapes=[
            vmem((96, 64, 384), BF16), vmem((6144, 128), F32), vmem((6144, 128), F32), vmem((6144, 128), F32),
            vmem((6144, 384), BF16),
            vmem((16, 3, 384, 128), BF16), vmem((16, 4, 96, 512), BF16), vmem((1024, 6144), BF16),
            vmem((1024, 384), F32), vmem((1024, 512), F32), vmem((NV, 96, 1024), BF16),
            vmem((NV, 96, 1024), F32), vmem((NV, 96, 1024), BF16), vmem((384, 1024), BF16),
            dma((N_SEMS,)), dma((N_SEMS,)), dma((3, 4)), dma((3, 4)), dma((3, 8)), dma((3, 8)), dma((12,)),
        ],
        compiler_params=pltpu.CompilerParams(collective_id=0, has_side_effects=True, vmem_limit_bytes=60 << 20),
    )(amplitudes[0], shard, labels, block)
    r = pl.pallas_call(
        cycle_kernel,
        name="cycle",
        out_shape=jax.ShapeDtypeStruct((6144, 384), BF16),
        in_specs=[any_spec, any_spec, any_spec],
        out_specs=vmem_spec,
        scratch_shapes=[
            vmem((1024, 6144), BF16), vmem((6144, 1024), BF16), vmem((384, 1024), BF16), vmem((384, 1024), BF16),
            vmem((1024, 384), BF16), vmem((1024, 384), BF16),
            dma((N_SEMS,)), dma((N_SEMS,)), dma((2, 3)), dma((2, 3)), dma((6,)),
        ],
        compiler_params=pltpu.CompilerParams(collective_id=1, has_side_effects=True, vmem_limit_bytes=60 << 20),
    )(bg, f, bv)
    return jnp.transpose(r.reshape(64, 96, 384), (1, 0, 2))[None]


def solution(mesh):
    in_specs = (P("occ", "vir", None, None), P("vir", None, "occ"), P(), P())
    out_specs = P("occ", "vir", None, None)
    return jax.shard_map(
        on_device, mesh=mesh, in_specs=in_specs, out_specs=out_specs, check_vma=False
    )
```

```python
import functools

import jax
import jax.numpy as jnp
from jax import lax
from jax.experimental import pallas as pl
from jax.experimental.pallas import tpu as pltpu
from jax.sharding import PartitionSpec as P

MESH = pl.DeviceIdType.MESH
NZ, NX, NY, NV = 8, 4, 2, 4
BF16, F32 = jnp.bfloat16, jnp.float32
GROUPS = ((0,), (1, 7), (2, 6), (3, 5), (4,))
COLUMNS = ((0,), (1, 3), (2,))
N_SEMS = 84


def position():
    o, v = lax.axis_index("occ"), lax.axis_index("vir")
    return o // (NX * NY), (o // NY) % NX, o % NY, v


def device(z, x, y, v):
    return ((z * NX + x) * NY + y, v)


def barrier(peers):
    sem = pltpu.get_barrier_semaphore()
    for peer in peers:
        pl.semaphore_signal(sem, 1, device_id=peer, device_id_type=MESH)
    pl.semaphore_wait(sem, len(peers))


def peers_of(z, x, y, v):
    ring = [
        device((z + 1) % NZ, x, y, v),
        device((z + NZ - 1) % NZ, x, y, v),
        device(z, (x + 1) % NX, y, v),
        device(z, (x + NX - 1) % NX, y, v),
        device(z, x, 1 - y, v),
    ]
    return ring + [device(z, x, y, (v + d) % NV) for d in range(1, NV)]


class Gather:
    def __init__(self, ref, block, region, two_pieces, send_sems, recv_sems):
        self.ref, self.block, self.region, self.two_pieces = ref, block, region, two_pieces
        self.send_sems, self.recv_sems = send_sems, recv_sems
        self.z, self.x, self.y, self.v = position()
        self.started = []

    def copy(self, key, z, x, half, piece):
        kind, d = key[0], key[1]
        if kind == "az":
            index = d * 4 + key[2]
        elif kind == "ax":
            index = 8 + (d * 8 + key[2]) * 2 + key[3]
        elif kind == "bx":
            index = 40 + d * 2 + key[2]
        else:
            index = 44 + (d * 4 + key[2]) * 4 + key[3]
        if piece == 1:
            index = 76 + {"az": 0, "ax": 1, "bx": 2, "bz": 3}[kind] * 2 + d
        (start, size), lanes = self.region(kind[0], half, piece)
        rows = pl.ds(pl.multiple_of((z % NZ * NX + x % NX) * self.block + start, 16), size)
        part = self.ref.at[rows, lanes]
        s = 1 - 2 * d
        if kind[1] == "z":
            target = device((self.z + s + NZ) % NZ, self.x, self.y, self.v)
        else:
            target = device(self.z, (self.x + s + NX) % NX, self.y, self.v)
        return pltpu.make_async_remote_copy(
            src_ref=part, dst_ref=part, send_sem=self.send_sems.at[index],
            recv_sem=self.recv_sems.at[index], device_id=target, device_id_type=MESH)

    def place(self, key, behind):
        kind, d = key[0], key[1]
        s = 1 - 2 * d
        half = None
        if kind == "az":
            dz, dx = -s * (key[2] + behind), 0
            half = d if key[2] == 3 else None
        elif kind == "ax":
            dz, dx = key[2], -s * (key[3] + behind)
            half = d if key[3] == 1 else None
        elif kind == "bx":
            dz, dx = 0, -s * (key[2] + behind)
            half = d if key[2] == 1 else None
        else:
            dz, dx = -s * (key[3] + behind), key[2]
            half = d if key[3] == 3 else None
        return self.z + dz + NZ, self.x + dx + NX, half

    def pieces(self, key):
        own = key[2:] in ((0,), (0, 0))
        if not own:
            return (None,)
        return (0, 1) if key[0][0] in self.two_pieces else (0,)

    def send(self, *key, piece=None):
        z, x, half = self.place(key, 0)
        self.copy(key, z, x, half, piece).start()
        self.started.append((key, piece))

    def wait(self, *key):
        z, x, half = self.place(key, 1)
        for piece in self.pieces(key):
            self.copy(key, z, x, half, piece).wait_recv()

    def own(self, piece):
        for kind in (("az", "bx"), ("ax", "bz")):
            for d in (0, 1):
                for name in kind:
                    key = (name, d, 0) if name in ("az", "bx") else (name, d, 0, 0)
                    if piece in self.pieces(key):
                        self.send(*key, piece=piece)

    def wave(self, w):
        both = (0, 1)
        if w <= 4:
            for d in both:
                self.wait("az", d, w - 1)
                if w <= 3:
                    self.send("az", d, w)
            for delta in GROUPS[w]:
                for d in both:
                    self.send("ax", d, delta, 0)
        if w == 1:
            for d in both:
                self.wait("bx", d, 0)
                self.send("bx", d, 1)
            for xi in COLUMNS[1]:
                for d in both:
                    self.send("bz", d, xi, 0)
        if w == 2:
            for d in both:
                self.wait("bx", d, 1)
            for d in both:
                self.send("bz", d, 2, 0)
        for delta in GROUPS[w - 1]:
            for d in both:
                self.wait("ax", d, delta, 0)
                self.send("ax", d, delta, 1)
        for u in range(3):
            t = w - 1 - u
            if 0 <= t <= 2:
                for xi in COLUMNS[u]:
                    for d in both:
                        self.wait("bz", d, xi, t)
                        self.send("bz", d, xi, t + 1)

    def settle(self, t, kinds="ab"):
        if "b" in kinds and t == 4:
            for xi in range(4):
                for d in (0, 1):
                    self.wait("bz", d, xi, 3)
        if "a" in kinds:
            for delta in GROUPS[t]:
                for d in (0, 1):
                    self.wait("ax", d, delta, 1)

    def finish(self):
        for key, piece in self.started:
            z, x, half = self.place(key, 0)
            self.copy(key, z, x, half, piece).wait_send()


def kernel(t_hbm, b_ref, occ_ref, vir_ref, vrow_ref, r_hbm,
           r_v, tf0, tf1, tf2, cd, u, s, bg, acc, fpart, fown, frecv, bvt, labels,
           fg, wf, bvf, rsend, rrecv,
           g_send, g_recv, g2_send, g2_recv, t_send, t_recv, f_send, f_recv,
           w_send, w_recv, v_send, v_recv, r_sem, rr_sem, one):
    z, x, y, v = position()
    o = (z * NX + x) * NY + y
    load_t = pltpu.make_async_copy(t_hbm, r_v, one.at[0])
    load_t.start()
    own = pl.ds(pl.multiple_of(o * 16, 16), 16)

    def place_b(n, _):
        four = jnp.concatenate([b_ref[4 * n + m].astype(F32) for m in range(4)], axis=1)
        bg[own, pl.ds(pl.multiple_of(n * 384, 384), 384)] = four.astype(BF16)
        return 0

    lax.fori_loop(0, 16, place_b, 0)
    barrier(peers_of(z, x, y, v))

    def swap_copy(there):
        rows = pl.ds(pl.multiple_of((o - y + there) * 16, 16), 16)
        return pltpu.make_async_remote_copy(
            src_ref=bg.at[rows, :], dst_ref=bg.at[rows, :], send_sem=one.at[2], recv_sem=one.at[3],
            device_id=device(z, x, 1 - y, v), device_id_type=MESH)

    def region(kind, half, piece):
        if piece is not None:
            rows = ((y if piece == 0 else 1 - y) * 16, 16)
        elif half is not None:
            rows = (half * 16, 16)
        else:
            rows = (0, 32)
        return rows, pl.ds(0, 3712) if kind == "a" else pl.ds(3712, 6144 - 3712)

    swap_copy(y).start()
    gather = Gather(bg, 32, region, "ab", g_send, g_recv)
    gather.own(0)

    mine_label = occ_ref[o]
    vrow = vrow_ref[...]

    def label_row(k, _):
        labels[pl.ds(k, 1), :] = vrow ^ (occ_ref[k] ^ mine_label)
        return 0

    lax.fori_loop(0, 64, label_row, 0)
    load_t.wait()

    def mask_row(c, _):
        row = r_v[pl.ds(pl.multiple_of(c * 64, 64), 64), :].astype(F32)
        row = jnp.where(labels[...] == vir_ref[v * 96 + c], row, 0.0)
        for n, tf in enumerate((tf0, tf1, tf2)):
            tf[pl.ds(pl.multiple_of(c * 64, 64), 64), :] = row[:, 128 * n:128 * n + 128]
        return 0

    lax.fori_loop(0, 96, mask_row, 0)
    swap_copy(1 - y).wait_recv()
    gather.own(1)

    lane = lax.broadcasted_iota(jnp.int32, (96, 128), 1)

    def turn(g, _):
        k = g * 4
        rows = [[tf[pl.ds(k + m, 96, stride=64), :] for tf in (tf0, tf1, tf2)] for m in range(4)]
        for n in range(3):
            for m in range(3):
                packed = jnp.concatenate([rows[m][n], rows[3][n][32 * m:32 * m + 32]], axis=0)
                u[g, m, pl.ds(128 * n, 128), :] = packed.T.astype(BF16)
        for m in range(4):
            a, b, c = rows[m]
            into = pl.ds(pl.multiple_of((k + m) * 96, 96), 96)
            cd[into, pl.ds(0, 128)] = a.astype(BF16)
            cd[into, pl.ds(128, 128)] = jnp.where(
                lane < 32, pltpu.roll(a, 32, 1), pltpu.roll(b, 32, 1)).astype(BF16)
            cd[into, pl.ds(256, 128)] = jnp.where(
                lane < 64, pltpu.roll(b, 64, 1), pltpu.roll(c, 64, 1)).astype(BF16)
            cd[into, pl.ds(384, 128)] = pltpu.roll(c, 96, 1).astype(BF16)
        return 0

    def t_copy(d, sb, wait=False):
        other = (v + NV - d) % NV if wait else (v + d) % NV
        here = other if wait else v
        return pltpu.make_async_remote_copy(
            src_ref=u.at[pl.ds(4 * sb, 4), :, pl.ds(pl.multiple_of(other * 96, 96), 96), :],
            dst_ref=s.at[pl.ds(4 * sb, 4), pl.ds(0, 3), :, pl.ds(pl.multiple_of(here * 128, 128), 128)],
            send_sem=t_send.at[d - 1, sb], recv_sem=t_recv.at[d - 1, sb],
            device_id=device(z, x, y, other), device_id_type=MESH)

    for sb in range(4):
        lax.fori_loop(4 * sb, 4 * sb + 4, turn, 0)
        for d in range(1, NV):
            t_copy(d, sb).start()
    mine = pltpu.make_async_copy(
        u.at[:, :, pl.ds(pl.multiple_of(v * 96, 96), 96), :],
        s.at[:, pl.ds(0, 3), :, pl.ds(pl.multiple_of(v * 128, 128), 128)], one.at[0])
    mine.start()

    pairs = ((0, 1), (7, 2), (6, 3), (5, 4))

    def zrow(delta):
        return pl.multiple_of(((z + delta) % NZ) * 128, 128)

    def combine(g, _):
        for blk in range(NV):
            lanes = pl.ds(128 * blk, 128)
            got = [s[g, m, :, lanes].astype(F32) for m in range(3)]
            last = jnp.where(lane < 32, pltpu.roll(got[0], 32, 1), jnp.where(
                lane < 64, pltpu.roll(got[1], 64, 1), pltpu.roll(got[2], 96, 1)))
            for m, other in enumerate(got + [last]):
                straight = cd[pl.ds(pl.multiple_of((4 * g + m) * 96, 96), 96), lanes].astype(F32)
                s[g, m, :, lanes] = (2.0 * straight - other).astype(BF16)
        return 0

    def pick(n):
        for delta in pairs[n]:
            rows = pl.ds(zrow(delta), 128)
            four = bg[rows, pl.ds(pl.multiple_of((o // 4) * 384, 384), 384)]
            bvt[:, rows] = four.astype(F32).T.astype(BF16)

    def f_copy(d, delta, wait):
        lanes = pl.ds(zrow(delta), 128)
        other = (v + NV - d) % NV if wait else (v + d) % NV
        here = other if wait else v
        return pltpu.make_async_remote_copy(
            src_ref=fpart.at[other, :, lanes], dst_ref=frecv.at[here, :, lanes],
            send_sem=f_send.at[d - 1, delta], recv_sem=f_recv.at[d - 1, delta],
            device_id=device(z, x, y, other), device_id_type=MESH)

    def fit(n):
        starts = [zrow(delta) for delta in pairs[n]]

        def step(kb, _):
            lanes = pl.ds(pl.multiple_of(kb * 768, 768), 768)
            left = jnp.concatenate([bg[pl.ds(a, 128), lanes] for a in starts], axis=0)
            part = jnp.dot(left, s[pl.ds(kb * 2, 2)].reshape(768, 512), preferred_element_type=F32)
            acc[...] = jnp.where(kb == 0, 0.0, acc[...]) + part
            return 0

        lax.fori_loop(0, 8, step, 0)
        for m, delta in enumerate(pairs[n]):
            rows = pl.ds(zrow(delta), 128)
            turned = acc[pl.ds(128 * m, 128), :].T
            for blk in range(NV):
                part = turned[128 * blk:128 * blk + 96]
                fpart[blk, :, rows] = part.astype(BF16)
                fown[blk, :, rows] = part
            for d in range(1, NV):
                f_copy(d, delta, False).start()

    gather.wave(1)
    gather.wave(2)
    gather.wave(3)
    gather.settle(0)
    gather.settle(1)
    pick(0)
    gather.wave(4)
    gather.settle(2)
    pick(1)
    mine.wait()
    for sb in range(4):
        for d in range(1, NV):
            t_copy(d, sb, True).wait_recv()
    lax.fori_loop(0, 16, combine, 0)
    fit(0)
    gather.wave(5)
    fit(1)
    gather.settle(3)
    fit(2)
    gather.settle(4)
    fit(3)
    pick(2)
    pick(3)
    two = pl.ds(pl.multiple_of((o % 4 - y) * 96, 96), 192)
    same = pltpu.make_async_copy(bvt.at[two, :], bvf.at[pl.ds(pl.multiple_of(v * 192, 192), 192), :], one.at[0])
    same.start()

    for d in range(1, NV):
        for delta in range(NZ):
            f_copy(d, delta, True).wait_recv()
    total = fown[v]
    for d in range(1, NV):
        total = total + frecv[(v + NV - d) % NV].astype(F32)
    total = total.astype(BF16)
    block = pl.multiple_of((z * NX + x) * 128, 128)
    fg[pl.ds(block, 96), :] = total
    wf[pl.ds(pl.multiple_of(v * 96, 96), 96), :] = total

    swap = pltpu.make_async_remote_copy(
        src_ref=fg.at[pl.ds(block + 64, 32), :], dst_ref=fg.at[pl.ds(block + 96, 32), :],
        send_sem=one.at[4], recv_sem=one.at[5], device_id=device(z, x, 1 - y, v), device_id_type=MESH)
    swap.start()

    mate, across = v + 1 - 2 * (v % 2), (v + 2) % NV
    far = (mate + 2) % NV

    def share(ref, size, send_sems, recv_sems, step, blk):
        rows = pl.ds(pl.multiple_of(blk * size, size), size)
        return pltpu.make_async_remote_copy(
            src_ref=ref.at[rows, :], dst_ref=ref.at[rows, :], send_sem=send_sems.at[step], recv_sem=recv_sems.at[step],
            device_id=device(z, x, y, across if step == 1 else mate), device_id_type=MESH)

    def region2(kind, half, piece):
        if kind == "b":
            rows = (0, 64) if half is None else (32 * half, 32)
        elif piece is not None:
            rows = (64 + 32 * piece, 32)
        else:
            rows = (64, 64) if half is None else (64 + 32 * half, 32)
        return rows, pl.ds(0, 1024)

    again = Gather(fg, 128, region2, "a", g2_send, g2_recv)
    again.own(0)
    same.wait()
    shares = ((bvf, 192, v_send, v_recv), (wf, 96, w_send, w_recv))
    for share_args in shares:
        share(*share_args, 1, v).start()
        share(*share_args, 0, v).start()
    swap.wait_recv()
    again.own(1)
    for share_args in shares:
        share(*share_args, 1, across).wait_recv()
        share(*share_args, 2, across).start()
        if share_args is shares[0]:
            again.wave(1)
    share(*shares[0], 0, mate).wait_recv()
    share(*shares[0], 2, far).wait_recv()
    first, second, third = (cd.at[pl.ds(1024 * n, 1024), pl.ds(0, 384)] for n in range(3))
    for ref, which in ((second, 1 - y), (first, y)):
        whole = jnp.concatenate(
            [bvf[pl.ds(pl.multiple_of(blk * 192 + which * 96, 96), 96), :] for blk in range(NV)], axis=0)
        ref[...] = whole.astype(F32).T.astype(BF16)

    def direct(n, _):
        lanes = pl.ds(pl.multiple_of(n * 384, 384), 384)
        part = lax.dot_general(bg[:, lanes], third[...], (((0,), (0,)), ((), ())), preferred_element_type=F32)
        r_v[pl.ds(pl.multiple_of(n * 384, 384), 384), :] = part.astype(BF16)
        return 0

    def add(row, size, part):
        rows = pl.ds(pl.multiple_of(row, 32), size)
        r_v[rows, :] = (r_v[rows, :].astype(F32) + part).astype(BF16)

    def r_copy(delta):
        rows = pl.ds(pl.multiple_of(((z + delta) % NZ) * 256, 256), 256)
        return pltpu.make_async_remote_copy(
            src_ref=rsend.at[rows, :], dst_ref=rrecv.at[rows, :], send_sem=r_sem.at[delta],
            recv_sem=rr_sem.at[delta], device_id=device(z, x, 1 - y, v), device_id_type=MESH)

    def theirs(t):
        for delta in GROUPS[t]:
            zz = (z + delta) % NZ
            left = jnp.concatenate(
                [fg[pl.ds(pl.multiple_of(zz * 512 + 128 * m, 128), 64), :] for m in range(NX)], axis=0)
            part = jnp.dot(left, second[...], preferred_element_type=F32)
            rsend[pl.ds(pl.multiple_of(zz * 256, 256), 256), :] = part.astype(BF16)
            r_copy(delta).start()

    def ours(t):
        for delta in GROUPS[t]:
            zz = (z + delta) % NZ
            rows = pl.ds(pl.multiple_of(zz * 512, 512), 512)
            part = jnp.dot(fg[rows, :], first[...], preferred_element_type=F32)
            for m in range(NX):
                pair = (zz * NX + m) * NY
                add((pair + y) * 96, 96, part[128 * m:128 * m + 96])
                add((pair + 1 - y) * 96 + 64, 32, part[128 * m + 96:128 * m + 128])

    def arrived(t):
        for delta in GROUPS[t]:
            r_copy(delta).wait_recv()
            zz = (z + delta) % NZ
            for m in range(NX):
                got = rrecv[pl.ds(pl.multiple_of(zz * 256 + 64 * m, 64), 64), :].astype(F32)
                add(((zz * NX + m) * NY + 1 - y) * 96, 64, got)

    again.wave(2)
    theirs(0)
    share(*shares[1], 0, mate).wait_recv()
    share(*shares[1], 2, far).wait_recv()
    third[...] = wf[...].astype(F32).T.astype(BF16)
    lax.fori_loop(0, 4, direct, 0)
    again.wave(3)
    theirs(1)
    lax.fori_loop(4, 10, direct, 0)
    again.wave(4)
    theirs(2)
    lax.fori_loop(10, 16, direct, 0)
    again.settle(0, "a")
    ours(0)
    again.settle(1, "a")
    ours(1)
    again.wave(5)
    theirs(3)
    again.settle(4, "b")
    theirs(4)
    for t in range(2, 5):
        again.settle(t, "a")
        ours(t)
        arrived(t - 2)
    arrived(3)
    arrived(4)
    save = pltpu.make_async_copy(r_v, r_hbm, one.at[0])
    save.start()

    for d in range(1, NV):
        for delta in range(NZ):
            f_copy(d, delta, False).wait_send()
        for sb in range(4):
            t_copy(d, sb).wait_send()
    swap_copy(y).wait_send()
    gather.finish()
    swap.wait_send()
    for share_args in shares:
        for step in range(3):
            share(*share_args, step, across if step == 2 else v).wait_send()
    for delta in range(NZ):
        r_copy(delta).wait_send()
    again.finish()
    save.wait()


def on_device(amplitudes, aux_ints, occ_irrep, vir_irrep):
    any_spec = pl.BlockSpec(memory_space=pl.ANY)
    vmem_spec = pl.BlockSpec(memory_space=pltpu.VMEM)
    smem_spec = pl.BlockSpec(memory_space=pltpu.SMEM)
    dma, vmem = pltpu.SemaphoreType.DMA, pltpu.VMEM
    r = pl.pallas_call(
        kernel,
        name="ccsd",
        out_shape=jax.ShapeDtypeStruct((6144, 384), BF16),
        in_specs=[any_spec, vmem_spec, smem_spec, smem_spec, vmem_spec],
        out_specs=any_spec,
        scratch_shapes=[
            vmem((6144, 384), BF16), vmem((6144, 128), F32), vmem((6144, 128), F32), vmem((6144, 128), F32),
            vmem((6144, 512), BF16), vmem((16, 3, 384, 128), BF16), vmem((16, 4, 96, 512), BF16),
            vmem((1024, 6144), BF16), vmem((256, 512), F32), vmem((NV, 96, 1024), BF16),
            vmem((NV, 96, 1024), F32), vmem((NV, 96, 1024), BF16), vmem((384, 1024), BF16),
            vmem((64, 384), jnp.int32),
            vmem((4096, 1024), BF16), vmem((384, 1024), BF16), vmem((768, 1024), BF16),
            vmem((2048, 384), BF16), vmem((2048, 384), BF16),
            dma((N_SEMS,)), dma((N_SEMS,)), dma((N_SEMS,)), dma((N_SEMS,)),
            dma((3, 4)), dma((3, 4)), dma((3, 8)), dma((3, 8)),
            dma((3,)), dma((3,)), dma((3,)), dma((3,)), dma((8,)), dma((8,)), dma((6,)),
        ],
        compiler_params=pltpu.CompilerParams(collective_id=0, has_side_effects=True, vmem_limit_bytes=63 << 20),
    )(amplitudes.reshape(6144, 384), jnp.transpose(aux_ints, (1, 2, 0)), occ_irrep, vir_irrep, vir_irrep[None, :])
    return jnp.transpose(r.reshape(64, 96, 384), (1, 0, 2))[None]


def solution(mesh):
    in_specs = (P("occ", "vir", None, None), P("vir", None, "occ"), P(), P())
    out_specs = P("occ", "vir", None, None)
    return jax.shard_map(
        on_device, mesh=mesh, in_specs=in_specs, out_specs=out_specs, check_vma=False
    )
```

```python
import functools

import jax
import jax.numpy as jnp
from jax import lax
from jax.experimental import pallas as pl
from jax.experimental.pallas import tpu as pltpu
from jax.sharding import PartitionSpec as P

MESH = pl.DeviceIdType.MESH
NZ, NX, NY, NV = 8, 4, 2, 4
BF16, F32 = jnp.bfloat16, jnp.float32
GROUPS = ((0,), (1, 7), (2, 6), (3, 5), (4,))
COLUMNS = ((0,), (1, 3), (2,))
N_SEMS = 84


def position():
    o, v = lax.axis_index("occ"), lax.axis_index("vir")
    return o // (NX * NY), (o // NY) % NX, o % NY, v


def device(z, x, y, v):
    return ((z * NX + x) * NY + y, v)


def barrier(peers):
    sem = pltpu.get_barrier_semaphore()
    for peer in peers:
        pl.semaphore_signal(sem, 1, device_id=peer, device_id_type=MESH)
    pl.semaphore_wait(sem, len(peers))


def peers_of(z, x, y, v):
    ring = [
        device((z + 1) % NZ, x, y, v),
        device((z + NZ - 1) % NZ, x, y, v),
        device(z, (x + 1) % NX, y, v),
        device(z, (x + NX - 1) % NX, y, v),
        device(z, x, 1 - y, v),
    ]
    return ring + [device(z, x, y, (v + d) % NV) for d in range(1, NV)]


class Gather:
    def __init__(self, ref, block, region, two_pieces, send_sems, recv_sems):
        self.ref, self.block, self.region, self.two_pieces = ref, block, region, two_pieces
        self.send_sems, self.recv_sems = send_sems, recv_sems
        self.z, self.x, self.y, self.v = position()
        self.started = []

    def copy(self, key, z, x, half, piece):
        kind, d = key[0], key[1]
        if kind == "az":
            index = d * 4 + key[2]
        elif kind == "ax":
            index = 8 + (d * 8 + key[2]) * 2 + key[3]
        elif kind == "bx":
            index = 40 + d * 2 + key[2]
        else:
            index = 44 + (d * 4 + key[2]) * 4 + key[3]
        if piece == 1:
            index = 76 + {"az": 0, "ax": 1, "bx": 2, "bz": 3}[kind] * 2 + d
        (start, size), lanes = self.region(kind[0], half, piece)
        rows = pl.ds(pl.multiple_of((z % NZ * NX + x % NX) * self.block + start, 16), size)
        part = self.ref.at[rows, lanes]
        s = 1 - 2 * d
        if kind[1] == "z":
            target = device((self.z + s + NZ) % NZ, self.x, self.y, self.v)
        else:
            target = device(self.z, (self.x + s + NX) % NX, self.y, self.v)
        return pltpu.make_async_remote_copy(
            src_ref=part, dst_ref=part, send_sem=self.send_sems.at[index],
            recv_sem=self.recv_sems.at[index], device_id=target, device_id_type=MESH)

    def place(self, key, behind):
        kind, d = key[0], key[1]
        s = 1 - 2 * d
        half = None
        if kind == "az":
            dz, dx = -s * (key[2] + behind), 0
            half = d if key[2] == 3 else None
        elif kind == "ax":
            dz, dx = key[2], -s * (key[3] + behind)
            half = d if key[3] == 1 else None
        elif kind == "bx":
            dz, dx = 0, -s * (key[2] + behind)
            half = d if key[2] == 1 else None
        else:
            dz, dx = -s * (key[3] + behind), key[2]
            half = d if key[3] == 3 else None
        return self.z + dz + NZ, self.x + dx + NX, half

    def pieces(self, key):
        own = key[2:] in ((0,), (0, 0))
        if not own:
            return (None,)
        return (0, 1) if key[0][0] in self.two_pieces else (0,)

    def send(self, *key, piece=None):
        z, x, half = self.place(key, 0)
        self.copy(key, z, x, half, piece).start()
        self.started.append((key, piece))

    def wait(self, *key):
        z, x, half = self.place(key, 1)
        for piece in self.pieces(key):
            self.copy(key, z, x, half, piece).wait_recv()

    def own(self, piece):
        for kind in (("az", "bx"), ("ax", "bz")):
            for d in (0, 1):
                for name in kind:
                    key = (name, d, 0) if name in ("az", "bx") else (name, d, 0, 0)
                    if piece in self.pieces(key):
                        self.send(*key, piece=piece)

    def wave(self, w):
        both = (0, 1)
        if w <= 4:
            for d in both:
                self.wait("az", d, w - 1)
                if w <= 3:
                    self.send("az", d, w)
            for delta in GROUPS[w]:
                for d in both:
                    self.send("ax", d, delta, 0)
        if w == 1:
            for d in both:
                self.wait("bx", d, 0)
                self.send("bx", d, 1)
            for xi in COLUMNS[1]:
                for d in both:
                    self.send("bz", d, xi, 0)
        if w == 2:
            for d in both:
                self.wait("bx", d, 1)
            for d in both:
                self.send("bz", d, 2, 0)
        for delta in GROUPS[w - 1]:
            for d in both:
                self.wait("ax", d, delta, 0)
                self.send("ax", d, delta, 1)
        for u in range(3):
            t = w - 1 - u
            if 0 <= t <= 2:
                for xi in COLUMNS[u]:
                    for d in both:
                        self.wait("bz", d, xi, t)
                        self.send("bz", d, xi, t + 1)

    def settle_a(self, t):
        for delta in GROUPS[t]:
            for d in (0, 1):
                self.wait("ax", d, delta, 1)

    def settle_b(self, u):
        for xi in COLUMNS[u]:
            for d in (0, 1):
                self.wait("bz", d, xi, 3)

    def finish(self):
        for key, piece in self.started:
            z, x, half = self.place(key, 0)
            self.copy(key, z, x, half, piece).wait_send()


def kernel(t_hbm, b_ref, occ_ref, vir_ref, vrow_ref, r_hbm,
           r_v, tf0, tf1, tf2, cd, u, s, bg, acc, fpart, fown, frecv, bvt, labels,
           fg, wf, bvf, rsend, rrecv,
           g_send, g_recv, g2_send, g2_recv, t_send, t_recv, f_send, f_recv,
           w_send, w_recv, v_send, v_recv, r_sem, rr_sem, one):
    z, x, y, v = position()
    o = (z * NX + x) * NY + y
    load_t = pltpu.make_async_copy(t_hbm, r_v, one.at[0])
    load_t.start()
    own = pl.ds(pl.multiple_of(o * 16, 16), 16)

    def place_b(n, _):
        four = jnp.concatenate([b_ref[4 * n + m].astype(F32) for m in range(4)], axis=1)
        bg[own, pl.ds(pl.multiple_of(n * 384, 384), 384)] = four.astype(BF16)
        return 0

    lax.fori_loop(0, 16, place_b, 0)
    barrier(peers_of(z, x, y, v))

    def swap_copy(there):
        rows = pl.ds(pl.multiple_of((o - y + there) * 16, 16), 16)
        return pltpu.make_async_remote_copy(
            src_ref=bg.at[rows, :], dst_ref=bg.at[rows, :], send_sem=one.at[2], recv_sem=one.at[3],
            device_id=device(z, x, 1 - y, v), device_id_type=MESH)

    def region(kind, half, piece):
        if piece is not None:
            rows = ((y if piece == 0 else 1 - y) * 16, 16)
        elif half is not None:
            rows = (half * 16, 16)
        else:
            rows = (0, 32)
        return rows, pl.ds(0, 3712) if kind == "a" else pl.ds(3712, 6144 - 3712)

    swap_copy(y).start()
    gather = Gather(bg, 32, region, "ab", g_send, g_recv)
    gather.own(0)

    mine_label = occ_ref[o]
    vrow = vrow_ref[...]

    def label_row(k, _):
        labels[pl.ds(k, 1), :] = vrow ^ (occ_ref[k] ^ mine_label)
        return 0

    lax.fori_loop(0, 64, label_row, 0)
    load_t.wait()

    def mask_row(c, _):
        row = r_v[pl.ds(pl.multiple_of(c * 64, 64), 64), :].astype(F32)
        row = jnp.where(labels[...] == vir_ref[v * 96 + c], row, 0.0)
        for n, tf in enumerate((tf0, tf1, tf2)):
            tf[pl.ds(pl.multiple_of(c * 64, 64), 64), :] = row[:, 128 * n:128 * n + 128]
        return 0

    lax.fori_loop(0, 96, mask_row, 0, unroll=4)
    swap_copy(1 - y).wait_recv()
    gather.own(1)

    lane = lax.broadcasted_iota(jnp.int32, (96, 128), 1)

    def turn(g, _):
        k = g * 4
        rows = [[tf[pl.ds(k + m, 96, stride=64), :] for tf in (tf0, tf1, tf2)] for m in range(4)]
        for n in range(3):
            for m in range(3):
                packed = jnp.concatenate([rows[m][n], rows[3][n][32 * m:32 * m + 32]], axis=0)
                u[g, m, pl.ds(128 * n, 128), :] = packed.T.astype(BF16)
        for m in range(4):
            a, b, c = rows[m]
            into = pl.ds(pl.multiple_of((k + m) * 96, 96), 96)
            cd[into, pl.ds(0, 128)] = a.astype(BF16)
            cd[into, pl.ds(128, 128)] = jnp.where(
                lane < 32, pltpu.roll(a, 32, 1), pltpu.roll(b, 32, 1)).astype(BF16)
            cd[into, pl.ds(256, 128)] = jnp.where(
                lane < 64, pltpu.roll(b, 64, 1), pltpu.roll(c, 64, 1)).astype(BF16)
            cd[into, pl.ds(384, 128)] = pltpu.roll(c, 96, 1).astype(BF16)
        return 0

    def t_copy(d, sb, wait=False):
        other = (v + NV - d) % NV if wait else (v + d) % NV
        here = other if wait else v
        return pltpu.make_async_remote_copy(
            src_ref=u.at[pl.ds(4 * sb, 4), :, pl.ds(pl.multiple_of(other * 96, 96), 96), :],
            dst_ref=s.at[pl.ds(4 * sb, 4), pl.ds(0, 3), :, pl.ds(pl.multiple_of(here * 128, 128), 128)],
            send_sem=t_send.at[d - 1, sb], recv_sem=t_recv.at[d - 1, sb],
            device_id=device(z, x, y, other), device_id_type=MESH)

    def hand_over(sb):
        lax.fori_loop(4 * sb, 4 * sb + 4, turn, 0)
        for d in range(1, NV):
            t_copy(d, sb).start()

    mine = pltpu.make_async_copy(
        u.at[:, :, pl.ds(pl.multiple_of(v * 96, 96), 96), :],
        s.at[:, pl.ds(0, 3), :, pl.ds(pl.multiple_of(v * 128, 128), 128)], one.at[0])
    pairs = ((0, 1), (7, 2), (6, 3), (5, 4))

    def zrow(delta):
        return pl.multiple_of(((z + delta) % NZ) * 128, 128)

    def combine_group(g, _):
        for blk in range(NV):
            lanes = pl.ds(128 * blk, 128)
            got = [s[g, m, :, lanes].astype(F32) for m in range(3)]
            last = jnp.where(lane < 32, pltpu.roll(got[0], 32, 1), jnp.where(
                lane < 64, pltpu.roll(got[1], 64, 1), pltpu.roll(got[2], 96, 1)))
            for m, other in enumerate(got + [last]):
                straight = cd[pl.ds(pl.multiple_of((4 * g + m) * 96, 96), 96), lanes].astype(F32)
                s[g, m, :, lanes] = (2.0 * straight - other).astype(BF16)
        return 0

    def combine(sb):
        for d in range(1, NV):
            t_copy(d, sb, True).wait_recv()
        lax.fori_loop(4 * sb, 4 * sb + 4, combine_group, 0)

    def pick(n):
        for delta in pairs[n]:
            rows = pl.ds(zrow(delta), 128)
            four = bg[rows, pl.ds(pl.multiple_of((o // 4) * 384, 384), 384)]
            bvt[:, rows] = four.astype(F32).T.astype(BF16)

    def f_copy(d, delta, wait):
        lanes = pl.ds(zrow(delta), 128)
        other = (v + NV - d) % NV if wait else (v + d) % NV
        here = other if wait else v
        return pltpu.make_async_remote_copy(
            src_ref=fpart.at[other, :, lanes], dst_ref=frecv.at[here, :, lanes],
            send_sem=f_send.at[d - 1, delta], recv_sem=f_recv.at[d - 1, delta],
            device_id=device(z, x, y, other), device_id_type=MESH)

    def fit(n, low, high):
        starts = [zrow(delta) for delta in pairs[n]]
        total = acc.at[pl.ds(256 * n, 256), :]

        def step(kb, _):
            lanes = pl.ds(pl.multiple_of(kb * 768, 768), 768)
            left = jnp.concatenate([bg[pl.ds(a, 128), lanes] for a in starts], axis=0)
            part = jnp.dot(left, s[pl.ds(kb * 2, 2)].reshape(768, 512), preferred_element_type=F32)
            total[...] = jnp.where(kb == 0, 0.0, total[...]) + part
            return 0

        lax.fori_loop(2 * low, 2 * high, step, 0)

    def reduce(n):
        for m, delta in enumerate(pairs[n]):
            rows = pl.ds(zrow(delta), 128)
            turned = acc[pl.ds(256 * n + 128 * m, 128), :].T
            for blk in range(NV):
                part = turned[128 * blk:128 * blk + 96]
                fpart[blk, :, rows] = part.astype(BF16)
                fown[blk, :, rows] = part
            for d in range(1, NV):
                f_copy(d, delta, False).start()

    hand_over(0)
    gather.wave(1)
    hand_over(1)
    gather.wave(2)
    hand_over(2)
    hand_over(3)
    mine.start()
    gather.wave(3)
    gather.settle_a(0)
    gather.settle_a(1)
    pick(0)
    mine.wait()
    combine(0)
    combine(1)
    fit(0, 0, 2)
    gather.wave(4)
    gather.settle_a(2)
    pick(1)
    combine(2)
    fit(0, 2, 3)
    fit(1, 0, 3)
    gather.wave(5)
    combine(3)
    fit(0, 3, 4)
    reduce(0)
    fit(1, 3, 4)
    reduce(1)
    gather.settle_a(3)
    fit(2, 0, 4)
    reduce(2)
    gather.settle_a(4)
    for column in range(3):
        gather.settle_b(column)
    fit(3, 0, 4)
    reduce(3)
    pick(2)
    pick(3)
    two = pl.ds(pl.multiple_of((o % 4 - y) * 96, 96), 192)
    same = pltpu.make_async_copy(bvt.at[two, :], bvf.at[pl.ds(pl.multiple_of(v * 192, 192), 192), :], one.at[0])
    same.start()

    for d in range(1, NV):
        for delta in range(NZ):
            f_copy(d, delta, True).wait_recv()
    total = fown[v]
    for d in range(1, NV):
        total = total + frecv[(v + NV - d) % NV].astype(F32)
    total = total.astype(BF16)
    block = pl.multiple_of((z * NX + x) * 128, 128)
    fg[pl.ds(block, 96), :] = total
    wf[pl.ds(pl.multiple_of(v * 96, 96), 96), :] = total

    swap = pltpu.make_async_remote_copy(
        src_ref=fg.at[pl.ds(block + 64, 32), :], dst_ref=fg.at[pl.ds(block + 96, 32), :],
        send_sem=one.at[4], recv_sem=one.at[5], device_id=device(z, x, 1 - y, v), device_id_type=MESH)
    swap.start()

    mate, across = v + 1 - 2 * (v % 2), (v + 2) % NV
    far = (mate + 2) % NV

    def share(ref, size, send_sems, recv_sems, step, blk):
        rows = pl.ds(pl.multiple_of(blk * size, size), size)
        return pltpu.make_async_remote_copy(
            src_ref=ref.at[rows, :], dst_ref=ref.at[rows, :], send_sem=send_sems.at[step], recv_sem=recv_sems.at[step],
            device_id=device(z, x, y, across if step == 1 else mate), device_id_type=MESH)

    def region2(kind, half, piece):
        if kind == "b":
            rows = (0, 64) if half is None else (32 * half, 32)
        elif piece is not None:
            rows = (64 + 32 * piece, 32)
        else:
            rows = (64, 64) if half is None else (64 + 32 * half, 32)
        return rows, pl.ds(0, 1024)

    again = Gather(fg, 128, region2, "a", g2_send, g2_recv)
    again.own(0)
    same.wait()
    shares = ((bvf, 192, v_send, v_recv), (wf, 96, w_send, w_recv))
    for share_args in shares:
        share(*share_args, 1, v).start()
        share(*share_args, 0, v).start()
    swap.wait_recv()
    again.own(1)
    for share_args in shares:
        share(*share_args, 1, across).wait_recv()
        share(*share_args, 2, across).start()
        if share_args is shares[0]:
            again.wave(1)
    share(*shares[0], 0, mate).wait_recv()
    share(*shares[0], 2, far).wait_recv()
    first, second, third = (cd.at[pl.ds(1024 * n, 1024), pl.ds(0, 384)] for n in range(3))
    for ref, which in ((second, 1 - y), (first, y)):
        whole = jnp.concatenate(
            [bvf[pl.ds(pl.multiple_of(blk * 192 + which * 96, 96), 96), :] for blk in range(NV)], axis=0)
        ref[...] = whole.astype(F32).T.astype(BF16)

    def direct(n, _):
        lanes = pl.ds(pl.multiple_of(n * 384, 384), 384)
        part = lax.dot_general(bg[:, lanes], third[...], (((0,), (0,)), ((), ())), preferred_element_type=F32)
        r_v[pl.ds(pl.multiple_of(n * 384, 384), 384), :] = part.astype(BF16)
        return 0

    def add(row, size, part):
        rows = pl.ds(pl.multiple_of(row, 32), size)
        r_v[rows, :] = (r_v[rows, :].astype(F32) + part).astype(BF16)

    def spot(delta, xi):
        return (z + delta) % NZ * NX + (x + xi) % NX

    def r_copy(delta, xi):
        rows = pl.ds(pl.multiple_of(spot(delta, xi) * 64, 64), 64)
        return pltpu.make_async_remote_copy(
            src_ref=rsend.at[rows, :], dst_ref=rrecv.at[rows, :], send_sem=r_sem.at[delta * NX + xi],
            recv_sem=rr_sem.at[delta * NX + xi], device_id=device(z, x, 1 - y, v), device_id_type=MESH)

    def front(w):
        return [(delta, xi) for u in range(3) for xi in COLUMNS[u] if 0 <= w - u <= 4 for delta in GROUPS[w - u]]

    def early_rows(w):
        return jnp.concatenate(
            [fg[pl.ds(pl.multiple_of(spot(*at) * 128, 128), 64), :] for at in front(w)], axis=0)

    def theirs(w):
        part = jnp.dot(early_rows(w), second[...], preferred_element_type=F32).astype(BF16)
        for n, at in enumerate(front(w)):
            rsend[pl.ds(pl.multiple_of(spot(*at) * 64, 64), 64), :] = part[64 * n:64 * n + 64]
            r_copy(*at).start()

    def ours_early(w):
        part = jnp.dot(early_rows(w), first[...], preferred_element_type=F32)
        for n, at in enumerate(front(w)):
            add((spot(*at) * NY + y) * 96, 64, part[64 * n:64 * n + 64])

    def ours_late(t):
        for delta in GROUPS[t]:
            left = jnp.concatenate(
                [fg[pl.ds(pl.multiple_of(spot(delta, m) * 128 + 64, 64), 64), :] for m in range(NX)], axis=0)
            part = jnp.dot(left, first[...], preferred_element_type=F32)
            for m in range(NX):
                pair = spot(delta, m) * NY
                add((pair + y) * 96 + 64, 32, part[64 * m:64 * m + 32])
                add((pair + 1 - y) * 96 + 64, 32, part[64 * m + 32:64 * m + 64])

    def arrived(w):
        for at in front(w):
            r_copy(*at).wait_recv()
            got = rrecv[pl.ds(pl.multiple_of(spot(*at) * 64, 64), 64), :].astype(F32)
            add((spot(*at) * NY + 1 - y) * 96, 64, got)

    theirs(0)
    theirs(1)
    again.wave(2)
    theirs(2)
    share(*shares[1], 0, mate).wait_recv()
    share(*shares[1], 2, far).wait_recv()
    third[...] = wf[...].astype(F32).T.astype(BF16)
    lax.fori_loop(0, 8, direct, 0)
    again.wave(3)
    theirs(3)
    lax.fori_loop(8, 16, direct, 0)
    for w in range(4):
        ours_early(w)
    again.wave(4)
    again.settle_b(0)
    theirs(4)
    ours_early(4)
    for t in range(2):
        again.settle_a(t)
        ours_late(t)
    for w in range(3):
        arrived(w)
    again.wave(5)
    again.settle_b(1)
    theirs(5)
    ours_early(5)
    again.settle_a(2)
    ours_late(2)
    arrived(3)
    again.settle_b(2)
    theirs(6)
    ours_early(6)
    again.settle_a(3)
    ours_late(3)
    arrived(4)
    again.settle_a(4)
    ours_late(4)
    arrived(5)
    arrived(6)
    save = pltpu.make_async_copy(r_v, r_hbm, one.at[0])
    save.start()

    for d in range(1, NV):
        for delta in range(NZ):
            f_copy(d, delta, False).wait_send()
        for sb in range(4):
            t_copy(d, sb).wait_send()
    swap_copy(y).wait_send()
    gather.finish()
    swap.wait_send()
    for share_args in shares:
        for step in range(3):
            share(*share_args, step, across if step == 2 else v).wait_send()
    for delta in range(NZ):
        for xi in range(NX):
            r_copy(delta, xi).wait_send()
    again.finish()
    save.wait()


def on_device(amplitudes, aux_ints, occ_irrep, vir_irrep):
    any_spec = pl.BlockSpec(memory_space=pl.ANY)
    vmem_spec = pl.BlockSpec(memory_space=pltpu.VMEM)
    smem_spec = pl.BlockSpec(memory_space=pltpu.SMEM)
    dma, vmem = pltpu.SemaphoreType.DMA, pltpu.VMEM
    r = pl.pallas_call(
        kernel,
        name="ccsd",
        out_shape=jax.ShapeDtypeStruct((6144, 384), BF16),
        in_specs=[any_spec, vmem_spec, smem_spec, smem_spec, vmem_spec],
        out_specs=any_spec,
        scratch_shapes=[
            vmem((6144, 384), BF16), vmem((6144, 128), F32), vmem((6144, 128), F32), vmem((6144, 128), F32),
            vmem((6144, 512), BF16), vmem((16, 3, 384, 128), BF16), vmem((16, 4, 96, 512), BF16),
            vmem((1024, 6144), BF16), vmem((1024, 512), F32), vmem((NV, 96, 1024), BF16),
            vmem((NV, 96, 1024), F32), vmem((NV, 96, 1024), BF16), vmem((384, 1024), BF16),
            vmem((64, 384), jnp.int32),
            vmem((4096, 1024), BF16), vmem((384, 1024), BF16), vmem((768, 1024), BF16),
            vmem((2048, 384), BF16), vmem((2048, 384), BF16),
            dma((N_SEMS,)), dma((N_SEMS,)), dma((N_SEMS,)), dma((N_SEMS,)),
            dma((3, 4)), dma((3, 4)), dma((3, 8)), dma((3, 8)),
            dma((3,)), dma((3,)), dma((3,)), dma((3,)), dma((32,)), dma((32,)), dma((6,)),
        ],
        compiler_params=pltpu.CompilerParams(collective_id=0, has_side_effects=True, vmem_limit_bytes=63 << 20),
    )(amplitudes.reshape(6144, 384), jnp.transpose(aux_ints, (1, 2, 0)), occ_irrep, vir_irrep, vir_irrep[None, :])
    return jnp.transpose(r.reshape(64, 96, 384), (1, 0, 2))[None]


def solution(mesh):
    in_specs = (P("occ", "vir", None, None), P("vir", None, "occ"), P(), P())
    out_specs = P("occ", "vir", None, None)
    return jax.shard_map(
        on_device, mesh=mesh, in_specs=in_specs, out_specs=out_specs, check_vma=False
    )
```

```python
import functools

import jax
import jax.numpy as jnp
from jax import lax
from jax.experimental import pallas as pl
from jax.experimental.pallas import tpu as pltpu
from jax.sharding import PartitionSpec as P

MESH = pl.DeviceIdType.MESH
NZ, NX, NY, NV = 8, 4, 2, 4
BF16, F32 = jnp.bfloat16, jnp.float32
GROUPS = ((0,), (1, 7), (2, 6), (3, 5), (4,))
COLUMNS = ((0,), (1, 3), (2,))
N_SEMS = 100


def position():
    o, v = lax.axis_index("occ"), lax.axis_index("vir")
    return o // (NX * NY), (o // NY) % NX, o % NY, v


def device(z, x, y, v):
    return ((z * NX + x) * NY + y, v)


def barrier(peers):
    sem = pltpu.get_barrier_semaphore()
    for peer in peers:
        pl.semaphore_signal(sem, 1, device_id=peer, device_id_type=MESH)
    pl.semaphore_wait(sem, len(peers))


def peers_of(z, x, y, v):
    ring = [
        device((z + 1) % NZ, x, y, v),
        device((z + NZ - 1) % NZ, x, y, v),
        device(z, (x + 1) % NX, y, v),
        device(z, (x + NX - 1) % NX, y, v),
        device(z, x, 1 - y, v),
    ]
    return ring + [device(z, x, y, (v + d) % NV) for d in range(1, NV)]


class Gather:
    def __init__(self, ref, block, region, two_pieces, far, send_sems, recv_sems):
        self.ref, self.block, self.region, self.two_pieces, self.far = ref, block, region, two_pieces, far
        self.send_sems, self.recv_sems = send_sems, recv_sems
        self.z, self.x, self.y, self.v = position()
        self.started = []

    def copy(self, key, z, x, half, piece):
        kind, d = key[0], key[1]
        if kind == "az":
            index = d * 4 + key[2]
        elif kind == "ax":
            index = 8 + (d * 8 + key[2]) * 2 + key[3]
        elif kind == "bx":
            index = 40 + d * 2 + key[2]
        elif kind == "bz":
            index = 44 + (d * 4 + key[2]) * 4 + key[3]
        else:
            index = 84 + d * 8 + key[2]
        if piece == 1:
            index = 76 + {"az": 0, "ax": 1, "bx": 2, "bz": 3}[kind] * 2 + d
        if kind == "cx":
            (start, size), lanes = (48 - 16 * d, 16), pl.ds(0, self.ref.shape[1])
        elif self.far and kind == "bz" and key[2] == 2:
            (start, size), lanes = (0, 32) if half is None else (16 * half, 16), pl.ds(0, self.ref.shape[1])
        else:
            (start, size), lanes = self.region(kind[0], half, piece)
        rows = pl.ds(pl.multiple_of((z % NZ * NX + x % NX) * self.block + start, 16), size)
        part = self.ref.at[rows, lanes]
        s = 1 - 2 * d
        if kind[1] == "z":
            target = device((self.z + s + NZ) % NZ, self.x, self.y, self.v)
        else:
            target = device(self.z, (self.x + s + NX) % NX, self.y, self.v)
        return pltpu.make_async_remote_copy(
            src_ref=part, dst_ref=part, send_sem=self.send_sems.at[index],
            recv_sem=self.recv_sems.at[index], device_id=target, device_id_type=MESH)

    def place(self, key, behind):
        kind, d = key[0], key[1]
        s = 1 - 2 * d
        half = None
        if kind == "az":
            dz, dx = -s * (key[2] + behind), 0
            half = d if key[2] == 3 else None
        elif kind == "ax":
            dz, dx = key[2], -s * (key[3] + behind)
            half = d if key[3] == 1 else None
        elif kind == "bx":
            dz, dx = 0, -s * (key[2] + behind)
            half = d if key[2] == 1 else None
        elif kind == "bz":
            dz, dx = -s * (key[3] + behind), key[2]
            half = d if key[3] == 3 else None
        else:
            dz, dx = key[2], -s * (1 + behind)
        return self.z + dz + NZ, self.x + dx + NX, half

    def pieces(self, key):
        own = key[0] != "cx" and key[2:] in ((0,), (0, 0))
        if not own:
            return (None,)
        return (0, 1) if key[0][0] in self.two_pieces else (0,)

    def send(self, *key, piece=None):
        z, x, half = self.place(key, 0)
        self.copy(key, z, x, half, piece).start()
        self.started.append((key, piece))

    def wait(self, *key):
        z, x, half = self.place(key, 1)
        for piece in self.pieces(key):
            self.copy(key, z, x, half, piece).wait_recv()

    def own(self, piece):
        for kind in (("az", "bx"), ("ax", "bz")):
            for d in (0, 1):
                for name in kind:
                    key = (name, d, 0) if name in ("az", "bx") else (name, d, 0, 0)
                    if piece in self.pieces(key):
                        self.send(*key, piece=piece)

    def wave(self, w):
        both = (0, 1)
        if w <= 4:
            for d in both:
                self.wait("az", d, w - 1)
                if w <= 3:
                    self.send("az", d, w)
            for delta in GROUPS[w]:
                for d in both:
                    self.send("ax", d, delta, 0)
        if w == 1:
            for d in both:
                self.wait("bx", d, 0)
                self.send("bx", d, 1)
            for xi in COLUMNS[1]:
                for d in both:
                    self.send("bz", d, xi, 0)
        if w == 2:
            for d in both:
                self.wait("bx", d, 1)
            for d in both:
                self.send("bz", d, 2, 0)
        for delta in GROUPS[w - 1]:
            for d in both:
                self.wait("ax", d, delta, 0)
                self.send("ax", d, delta, 1)
        for u in range(3):
            t = w - 1 - u
            if 0 <= t <= 2:
                for xi in COLUMNS[u]:
                    for d in both:
                        self.wait("bz", d, xi, t)
                        self.send("bz", d, xi, t + 1)
                if u == 1:
                    self.send_far(t + 1)

    def send_far(self, t):
        if self.far:
            for delta in GROUPS[t]:
                for d in (0, 1):
                    self.send("cx", d, delta)

    def wait_far(self, t):
        for delta in GROUPS[t]:
            for d in (0, 1):
                self.wait("cx", d, delta)

    def settle_a(self, t):
        for delta in GROUPS[t]:
            for d in (0, 1):
                self.wait("ax", d, delta, 1)

    def settle_b(self, u):
        for xi in COLUMNS[u]:
            for d in (0, 1):
                self.wait("bz", d, xi, 3)
        if u == 1:
            self.send_far(4)

    def finish(self):
        for key, piece in self.started:
            z, x, half = self.place(key, 0)
            self.copy(key, z, x, half, piece).wait_send()


def kernel(t_hbm, b_ref, occ_ref, vir_ref, vrow_ref, r_hbm,
           r_v, tf0, tf1, tf2, cd, u, s, bg, acc, fpart, fown, frecv, bvt, labels,
           fg, wf, bvf, rsend, rrecv,
           g_send, g_recv, g2_send, g2_recv, t_send, t_recv, f_send, f_recv,
           w_send, w_recv, v_send, v_recv, r_sem, rr_sem, one):
    z, x, y, v = position()
    o = (z * NX + x) * NY + y
    load_t = pltpu.make_async_copy(t_hbm, r_v, one.at[0])
    load_t.start()
    own = pl.ds(pl.multiple_of(o * 16, 16), 16)

    def place_b(n, _):
        four = jnp.concatenate([b_ref[4 * n + m].astype(F32) for m in range(4)], axis=1)
        bg[own, pl.ds(pl.multiple_of(n * 384, 384), 384)] = four.astype(BF16)
        return 0

    lax.fori_loop(0, 16, place_b, 0)
    barrier(peers_of(z, x, y, v))

    def swap_copy(there):
        rows = pl.ds(pl.multiple_of((o - y + there) * 16, 16), 16)
        return pltpu.make_async_remote_copy(
            src_ref=bg.at[rows, :], dst_ref=bg.at[rows, :], send_sem=one.at[2], recv_sem=one.at[3],
            device_id=device(z, x, 1 - y, v), device_id_type=MESH)

    def region(kind, half, piece):
        if piece is not None:
            rows = ((y if piece == 0 else 1 - y) * 16, 16)
        elif half is not None:
            rows = (half * 16, 16)
        else:
            rows = (0, 32)
        return rows, pl.ds(0, 3712) if kind == "a" else pl.ds(3712, 6144 - 3712)

    swap_copy(y).start()
    gather = Gather(bg, 32, region, "ab", False, g_send, g_recv)
    gather.own(0)

    mine_label = occ_ref[o]
    vrow = vrow_ref[...].reshape(1, 384)

    def label_row(k, _):
        labels[pl.ds(k, 1), :] = vrow ^ (occ_ref[k] ^ mine_label)
        return 0

    lax.fori_loop(0, 64, label_row, 0)
    load_t.wait()

    def mask_row(c, _):
        row = r_v[pl.ds(pl.multiple_of(c * 64, 64), 64), :].astype(F32)
        row = jnp.where(labels[...] == vir_ref[v * 96 + c], row, 0.0)
        for n, tf in enumerate((tf0, tf1, tf2)):
            tf[pl.ds(pl.multiple_of(c * 64, 64), 64), :] = row[:, 128 * n:128 * n + 128]
        return 0

    lax.fori_loop(0, 96, mask_row, 0, unroll=4)
    swap_copy(1 - y).wait_recv()
    gather.own(1)

    lane = lax.broadcasted_iota(jnp.int32, (96, 128), 1)

    def turn(g, _):
        k = g * 4
        rows = [[tf[pl.ds(k + m, 96, stride=64), :] for tf in (tf0, tf1, tf2)] for m in range(4)]
        for n in range(3):
            for m in range(3):
                packed = jnp.concatenate([rows[m][n], rows[3][n][32 * m:32 * m + 32]], axis=0)
                u[g, m, pl.ds(128 * n, 128), :] = packed.T.astype(BF16)
        for m in range(4):
            a, b, c = rows[m]
            into = pl.ds(pl.multiple_of((k + m) * 96, 96), 96)
            cd[into, pl.ds(0, 128)] = a.astype(BF16)
            cd[into, pl.ds(128, 128)] = jnp.where(
                lane < 32, pltpu.roll(a, 32, 1), pltpu.roll(b, 32, 1)).astype(BF16)
            cd[into, pl.ds(256, 128)] = jnp.where(
                lane < 64, pltpu.roll(b, 64, 1), pltpu.roll(c, 64, 1)).astype(BF16)
            cd[into, pl.ds(384, 128)] = pltpu.roll(c, 96, 1).astype(BF16)
        return 0

    def t_copy(d, sb, wait=False):
        other = (v + NV - d) % NV if wait else (v + d) % NV
        here = other if wait else v
        return pltpu.make_async_remote_copy(
            src_ref=u.at[pl.ds(4 * sb, 4), :, pl.ds(pl.multiple_of(other * 96, 96), 96), :],
            dst_ref=s.at[pl.ds(4 * sb, 4), pl.ds(0, 3), :, pl.ds(pl.multiple_of(here * 128, 128), 128)],
            send_sem=t_send.at[d - 1, sb], recv_sem=t_recv.at[d - 1, sb],
            device_id=device(z, x, y, other), device_id_type=MESH)

    def hand_over(sb):
        lax.fori_loop(4 * sb, 4 * sb + 4, turn, 0)
        for d in range(1, NV):
            t_copy(d, sb).start()

    mine = pltpu.make_async_copy(
        u.at[:, :, pl.ds(pl.multiple_of(v * 96, 96), 96), :],
        s.at[:, pl.ds(0, 3), :, pl.ds(pl.multiple_of(v * 128, 128), 128)], one.at[0])
    pairs = ((0, 1), (7, 2), (6, 3), (5, 4))

    def zrow(delta):
        return pl.multiple_of(((z + delta) % NZ) * 128, 128)

    def combine_group(g, _):
        for blk in range(NV):
            lanes = pl.ds(128 * blk, 128)
            got = [s[g, m, :, lanes].astype(F32) for m in range(3)]
            last = jnp.where(lane < 32, pltpu.roll(got[0], 32, 1), jnp.where(
                lane < 64, pltpu.roll(got[1], 64, 1), pltpu.roll(got[2], 96, 1)))
            for m, other in enumerate(got + [last]):
                straight = cd[pl.ds(pl.multiple_of((4 * g + m) * 96, 96), 96), lanes].astype(F32)
                s[g, m, :, lanes] = (2.0 * straight - other).astype(BF16)
        return 0

    def combine(sb):
        for d in range(1, NV):
            t_copy(d, sb, True).wait_recv()
        lax.fori_loop(4 * sb, 4 * sb + 4, combine_group, 0)

    mate, across = v + 1 - 2 * (v % 2), (v + 2) % NV
    far = (mate + 2) % NV
    two = pl.ds(pl.multiple_of((o % 4 - y) * 96, 96), 192)

    def share_v(step, delta, blk):
        rows, lanes = pl.ds(pl.multiple_of(blk * 192, 192), 192), pl.ds(zrow(delta), 128)
        into = bvf.at[rows, lanes]
        return pltpu.make_async_remote_copy(
            src_ref=into if step == 2 else bvt.at[two, lanes], dst_ref=into,
            send_sem=v_send.at[step, delta], recv_sem=v_recv.at[step, delta],
            device_id=device(z, x, y, across if step == 1 else mate), device_id_type=MESH)

    def pick(n):
        for delta in pairs[n]:
            rows = pl.ds(zrow(delta), 128)
            four = bg[rows, pl.ds(pl.multiple_of((o // 4) * 384, 384), 384)]
            bvt[:, rows] = four.astype(F32).T.astype(BF16)

    def f_copy(d, delta, wait):
        lanes = pl.ds(zrow(delta), 128)
        other = (v + NV - d) % NV if wait else (v + d) % NV
        here = other if wait else v
        return pltpu.make_async_remote_copy(
            src_ref=fpart.at[other, :, lanes], dst_ref=frecv.at[here, :, lanes],
            send_sem=f_send.at[d - 1, delta], recv_sem=f_recv.at[d - 1, delta],
            device_id=device(z, x, y, other), device_id_type=MESH)

    def fit(n, low, high, fresh=False):
        starts = [zrow(delta) for delta in pairs[n]]
        total = acc.at[pl.ds(256 * n, 256), :]

        def step(kb, _):
            lanes = pl.ds(pl.multiple_of(kb * 768, 768), 768)
            left = jnp.concatenate([bg[pl.ds(a, 128), lanes] for a in starts], axis=0)
            part = jnp.dot(left, s[pl.ds(kb * 2, 2)].reshape(768, 512), preferred_element_type=F32)
            total[...] = (jnp.where(kb == low, 0.0, total[...]) if fresh else total[...]) + part
            return 0

        lax.fori_loop(low, high, step, 0)

    def reduce(n):
        for m, delta in enumerate(pairs[n]):
            rows = pl.ds(zrow(delta), 128)
            turned = acc[pl.ds(256 * n + 128 * m, 128), :].T
            for blk in range(NV):
                part = turned[128 * blk:128 * blk + 96]
                fpart[blk, :, rows] = part.astype(BF16)
                fown[blk, :, rows] = part
            for d in range(1, NV):
                f_copy(d, delta, False).start()

    hand_over(0)
    gather.wave(1)
    hand_over(1)
    gather.wave(2)
    hand_over(2)
    hand_over(3)
    mine.start()
    gather.wave(3)
    gather.settle_a(0)
    gather.settle_a(1)
    pick(0)
    mine.wait()
    combine(0)
    combine(1)
    fit(0, 0, 4, True)
    gather.wave(4)
    gather.settle_a(2)
    pick(1)
    for n in range(2):
        for delta in pairs[n]:
            share_v(1, delta, v).start()
            share_v(0, delta, v).start()
    combine(2)
    fit(0, 4, 6)
    fit(1, 0, 6, True)
    gather.wave(5)
    combine(3)
    fit(0, 6, 8)
    reduce(0)
    fit(1, 6, 8)
    reduce(1)
    fit(2, 5, 8, True)
    gather.settle_a(3)
    fit(2, 0, 5)
    reduce(2)
    for column in range(3):
        gather.settle_b(column)
    fit(3, 5, 8, True)
    gather.settle_a(4)
    fit(3, 0, 5)
    reduce(3)
    pick(2)
    pick(3)
    for n in range(2):
        for delta in pairs[n]:
            share_v(1, delta, across).wait_recv()
            share_v(2, delta, across).start()
    same = pltpu.make_async_copy(bvt.at[two, :], bvf.at[pl.ds(pl.multiple_of(v * 192, 192), 192), :], one.at[0])
    same.start()

    for d in range(1, NV):
        for delta in range(NZ):
            f_copy(d, delta, True).wait_recv()
    total = fown[v]
    for d in range(1, NV):
        total = total + frecv[(v + NV - d) % NV].astype(F32)
    total = total.astype(BF16)
    block = pl.multiple_of((z * NX + x) * 128, 128)
    fg[pl.ds(block, 96), :] = total
    wf[pl.ds(pl.multiple_of(v * 96, 96), 96), :] = total

    swap = pltpu.make_async_remote_copy(
        src_ref=fg.at[pl.ds(block + 64, 32), :], dst_ref=fg.at[pl.ds(block + 96, 32), :],
        send_sem=one.at[4], recv_sem=one.at[5], device_id=device(z, x, 1 - y, v), device_id_type=MESH)
    swap.start()

    def share_w(step, blk):
        rows = pl.ds(pl.multiple_of(blk * 96, 96), 96)
        return pltpu.make_async_remote_copy(
            src_ref=wf.at[rows, :], dst_ref=wf.at[rows, :], send_sem=w_send.at[step], recv_sem=w_recv.at[step],
            device_id=device(z, x, y, across if step == 1 else mate), device_id_type=MESH)

    def region2(kind, half, piece):
        if kind == "b":
            rows = (0, 64) if half is None else (32 * half, 32)
        elif piece is not None:
            rows = (64 + 32 * piece, 32)
        else:
            rows = (64, 64) if half is None else (64 + 32 * half, 32)
        return rows, pl.ds(0, 1024)

    again = Gather(fg, 128, region2, "a", True, g2_send, g2_recv)
    again.own(0)
    same.wait()
    late = pairs[2] + pairs[3]
    for delta in late:
        share_v(1, delta, v).start()
        share_v(0, delta, v).start()
    share_w(1, v).start()
    share_w(0, v).start()
    swap.wait_recv()
    again.own(1)
    for delta in late:
        share_v(1, delta, across).wait_recv()
        share_v(2, delta, across).start()
    again.wave(1)
    share_w(1, across).wait_recv()
    share_w(2, across).start()
    for delta in range(NZ):
        share_v(0, delta, mate).wait_recv()
        share_v(2, delta, far).wait_recv()
    first, second, third = (cd.at[pl.ds(1024 * n, 1024), pl.ds(0, 384)] for n in range(3))
    for ref, which in ((second, 1 - y), (first, y)):
        whole = jnp.concatenate(
            [bvf[pl.ds(pl.multiple_of(blk * 192 + which * 96, 96), 96), :] for blk in range(NV)], axis=0)
        ref[...] = whole.astype(F32).T.astype(BF16)

    def direct(n, _):
        lanes = pl.ds(pl.multiple_of(n * 384, 384), 384)
        part = lax.dot_general(bg[:, lanes], third[...], (((0,), (0,)), ((), ())), preferred_element_type=F32)
        r_v[pl.ds(pl.multiple_of(n * 384, 384), 384), :] = part.astype(BF16)
        return 0

    def add(row, size, part):
        rows = pl.ds(pl.multiple_of(row, 32), size)
        r_v[rows, :] = (r_v[rows, :].astype(F32) + part).astype(BF16)

    def spot(delta, xi):
        return (z + delta) % NZ * NX + (x + xi) % NX

    def r_copy(delta, xi):
        rows = pl.ds(pl.multiple_of(spot(delta, xi) * 64, 64), 64)
        return pltpu.make_async_remote_copy(
            src_ref=rsend.at[rows, :], dst_ref=rrecv.at[rows, :], send_sem=r_sem.at[delta * NX + xi],
            recv_sem=rr_sem.at[delta * NX + xi], device_id=device(z, x, 1 - y, v), device_id_type=MESH)

    def front(w):
        return [(delta, xi) for u in range(3) for xi in COLUMNS[u] if 0 <= w - u <= 4 for delta in GROUPS[w - u]]

    def early_rows(w):
        return jnp.concatenate(
            [fg[pl.ds(pl.multiple_of(spot(*at) * 128, 128), 64), :] for at in front(w)], axis=0)

    def theirs(w):
        part = jnp.dot(early_rows(w), second[...], preferred_element_type=F32).astype(BF16)
        for n, at in enumerate(front(w)):
            rsend[pl.ds(pl.multiple_of(spot(*at) * 64, 64), 64), :] = part[64 * n:64 * n + 64]
            r_copy(*at).start()

    def ours_early(w):
        part = jnp.dot(early_rows(w), first[...], preferred_element_type=F32)
        for n, at in enumerate(front(w)):
            add((spot(*at) * NY + y) * 96, 64, part[64 * n:64 * n + 64])

    def ours_late(t):
        for delta in GROUPS[t]:
            left = jnp.concatenate(
                [fg[pl.ds(pl.multiple_of(spot(delta, m) * 128 + 64, 64), 64), :] for m in range(NX)], axis=0)
            part = jnp.dot(left, first[...], preferred_element_type=F32)
            for m in range(NX):
                pair = spot(delta, m) * NY
                add((pair + y) * 96 + 64, 32, part[64 * m:64 * m + 32])
                add((pair + 1 - y) * 96 + 64, 32, part[64 * m + 32:64 * m + 64])

    def arrived(w):
        for at in front(w):
            r_copy(*at).wait_recv()
            got = rrecv[pl.ds(pl.multiple_of(spot(*at) * 64, 64), 64), :].astype(F32)
            add((spot(*at) * NY + 1 - y) * 96, 64, got)

    theirs(0)
    theirs(1)
    again.wave(2)
    theirs(2)
    share_w(0, mate).wait_recv()
    share_w(2, far).wait_recv()
    third[...] = wf[...].astype(F32).T.astype(BF16)
    lax.fori_loop(0, 8, direct, 0)
    again.wave(3)
    again.wait_far(1)
    theirs(3)
    lax.fori_loop(8, 16, direct, 0)
    for w in range(4):
        ours_early(w)
    again.wave(4)
    again.settle_b(0)
    again.wait_far(2)
    theirs(4)
    ours_early(4)
    for t in range(2):
        again.settle_a(t)
        ours_late(t)
    for w in range(3):
        arrived(w)
    again.wave(5)
    again.settle_b(1)
    again.wait_far(3)
    theirs(5)
    ours_early(5)
    again.settle_a(2)
    ours_late(2)
    arrived(3)
    again.settle_b(2)
    again.wait_far(4)
    theirs(6)
    ours_early(6)
    again.settle_a(3)
    ours_late(3)
    arrived(4)
    again.settle_a(4)
    ours_late(4)
    arrived(5)
    arrived(6)
    save = pltpu.make_async_copy(r_v, r_hbm, one.at[0])
    save.start()

    for d in range(1, NV):
        for delta in range(NZ):
            f_copy(d, delta, False).wait_send()
        for sb in range(4):
            t_copy(d, sb).wait_send()
    swap_copy(y).wait_send()
    gather.finish()
    swap.wait_send()
    for step in range(3):
        share_w(step, across if step == 2 else v).wait_send()
        for delta in range(NZ):
            share_v(step, delta, across if step == 2 else v).wait_send()
    for delta in range(NZ):
        for xi in range(NX):
            r_copy(delta, xi).wait_send()
    again.finish()
    save.wait()


def on_device(amplitudes, aux_ints, occ_irrep, vir_irrep):
    any_spec = pl.BlockSpec(memory_space=pl.ANY)
    vmem_spec = pl.BlockSpec(memory_space=pltpu.VMEM)
    smem_spec = pl.BlockSpec(memory_space=pltpu.SMEM)
    dma, vmem = pltpu.SemaphoreType.DMA, pltpu.VMEM
    r = pl.pallas_call(
        kernel,
        name="ccsd",
        out_shape=jax.ShapeDtypeStruct((6144, 384), BF16),
        in_specs=[any_spec, vmem_spec, smem_spec, smem_spec, vmem_spec],
        out_specs=any_spec,
        scratch_shapes=[
            vmem((6144, 384), BF16), vmem((6144, 128), F32), vmem((6144, 128), F32), vmem((6144, 128), F32),
            vmem((6144, 512), BF16), vmem((16, 3, 384, 128), BF16), vmem((16, 4, 96, 512), BF16),
            vmem((1024, 6144), BF16), vmem((1024, 512), F32), vmem((NV, 96, 1024), BF16),
            vmem((NV, 96, 1024), F32), vmem((NV, 96, 1024), BF16), vmem((384, 1024), BF16),
            vmem((64, 384), jnp.int32),
            vmem((4096, 1024), BF16), vmem((384, 1024), BF16), vmem((768, 1024), BF16),
            vmem((2048, 384), BF16), vmem((2048, 384), BF16),
            dma((N_SEMS,)), dma((N_SEMS,)), dma((N_SEMS,)), dma((N_SEMS,)),
            dma((3, 4)), dma((3, 4)), dma((3, 8)), dma((3, 8)),
            dma((3,)), dma((3,)), dma((3, 8)), dma((3, 8)), dma((32,)), dma((32,)), dma((6,)),
        ],
        compiler_params=pltpu.CompilerParams(collective_id=0, has_side_effects=True, vmem_limit_bytes=63 << 20),
    )(amplitudes.reshape(6144, 384), jnp.transpose(aux_ints, (1, 2, 0)), occ_irrep, vir_irrep, vir_irrep)
    return jnp.transpose(r.reshape(64, 96, 384), (1, 0, 2))[None]


def solution(mesh):
    in_specs = (P("occ", "vir", None, None), P("vir", None, "occ"), P(), P())
    out_specs = P("occ", "vir", None, None)
    return jax.shard_map(
        on_device, mesh=mesh, in_specs=in_specs, out_specs=out_specs, check_vma=False
    )
```

```python
import functools

import jax
import jax.numpy as jnp
from jax import lax
from jax.experimental import pallas as pl
from jax.experimental.pallas import tpu as pltpu
from jax.sharding import PartitionSpec as P

MESH = pl.DeviceIdType.MESH
NZ, NX, NY, NV = 8, 4, 2, 4
BF16, F32 = jnp.bfloat16, jnp.float32
GROUPS = ((0,), (1, 7), (2, 6), (3, 5), (4,))
COLUMNS = ((0,), (1, 3), (2,))
N_SEMS = 100


def position():
    o, v = lax.axis_index("occ"), lax.axis_index("vir")
    return o // (NX * NY), (o // NY) % NX, o % NY, v


def device(z, x, y, v):
    return ((z * NX + x) * NY + y, v)


def barrier(peers):
    sem = pltpu.get_barrier_semaphore()
    for peer in peers:
        pl.semaphore_signal(sem, 1, device_id=peer, device_id_type=MESH)
    pl.semaphore_wait(sem, len(peers))


def peers_of(z, x, y, v):
    ring = [
        device((z + 1) % NZ, x, y, v),
        device((z + NZ - 1) % NZ, x, y, v),
        device(z, (x + 1) % NX, y, v),
        device(z, (x + NX - 1) % NX, y, v),
        device(z, x, 1 - y, v),
    ]
    return ring + [device(z, x, y, (v + d) % NV) for d in range(1, NV)]


class Gather:
    def __init__(self, ref, base, block, region, two_pieces, far, send_sems, recv_sems):
        self.ref, self.base, self.block, self.region = ref, base, block, region
        self.two_pieces, self.far = two_pieces, far
        self.send_sems, self.recv_sems = send_sems, recv_sems
        self.z, self.x, self.y, self.v = position()
        self.started = []

    def copy(self, key, z, x, half, piece):
        kind, d = key[0], key[1]
        if kind == "az":
            index = d * 4 + key[2]
        elif kind == "ax":
            index = 8 + (d * 8 + key[2]) * 2 + key[3]
        elif kind == "bx":
            index = 40 + d * 2 + key[2]
        elif kind == "bz":
            index = 44 + (d * 4 + key[2]) * 4 + key[3]
        else:
            index = 84 + d * 8 + key[2]
        if piece == 1:
            index = 76 + {"az": 0, "ax": 1, "bx": 2, "bz": 3}[kind] * 2 + d
        (start, size), lanes = self.region("b" if kind == "cx" else kind[0], half, piece)
        if kind == "cx":
            start, size = 48 - 16 * d, 16
        elif self.far and kind == "bz" and key[2] == 2:
            start, size = (0, 32) if half is None else (16 * half, 16)
        rows = pl.ds(pl.multiple_of(self.base + (z % NZ * NX + x % NX) * self.block + start, 16), size)
        part = self.ref.at[rows, lanes]
        s = 1 - 2 * d
        if kind[1] == "z":
            target = device((self.z + s + NZ) % NZ, self.x, self.y, self.v)
        else:
            target = device(self.z, (self.x + s + NX) % NX, self.y, self.v)
        return pltpu.make_async_remote_copy(
            src_ref=part, dst_ref=part, send_sem=self.send_sems.at[index],
            recv_sem=self.recv_sems.at[index], device_id=target, device_id_type=MESH)

    def place(self, key, behind):
        kind, d = key[0], key[1]
        s = 1 - 2 * d
        half = None
        if kind == "az":
            dz, dx = -s * (key[2] + behind), 0
            half = d if key[2] == 3 else None
        elif kind == "ax":
            dz, dx = key[2], -s * (key[3] + behind)
            half = d if key[3] == 1 else None
        elif kind == "bx":
            dz, dx = 0, -s * (key[2] + behind)
            half = d if key[2] == 1 else None
        elif kind == "bz":
            dz, dx = -s * (key[3] + behind), key[2]
            half = d if key[3] == 3 else None
        else:
            dz, dx = key[2], -s * (1 + behind)
        return self.z + dz + NZ, self.x + dx + NX, half

    def pieces(self, key):
        own = key[0] != "cx" and key[2:] in ((0,), (0, 0))
        if not own:
            return (None,)
        return (0, 1) if key[0][0] in self.two_pieces else (0,)

    def send(self, *key, piece=None):
        z, x, half = self.place(key, 0)
        self.copy(key, z, x, half, piece).start()
        self.started.append((key, piece))

    def wait(self, *key):
        z, x, half = self.place(key, 1)
        for piece in self.pieces(key):
            self.copy(key, z, x, half, piece).wait_recv()

    def own(self, piece):
        for kind in (("az", "bx"), ("ax", "bz")):
            for d in (0, 1):
                for name in kind:
                    key = (name, d, 0) if name in ("az", "bx") else (name, d, 0, 0)
                    if piece in self.pieces(key):
                        self.send(*key, piece=piece)

    def wave(self, w):
        both = (0, 1)
        if w <= 4:
            for d in both:
                self.wait("az", d, w - 1)
                if w <= 3:
                    self.send("az", d, w)
            for delta in GROUPS[w]:
                for d in both:
                    self.send("ax", d, delta, 0)
        if w == 1:
            for d in both:
                self.wait("bx", d, 0)
                self.send("bx", d, 1)
            for xi in COLUMNS[1]:
                for d in both:
                    self.send("bz", d, xi, 0)
        if w == 2:
            for d in both:
                self.wait("bx", d, 1)
            for d in both:
                self.send("bz", d, 2, 0)
        for delta in GROUPS[w - 1]:
            for d in both:
                self.wait("ax", d, delta, 0)
                self.send("ax", d, delta, 1)
        for u in range(3):
            t = w - 1 - u
            if 0 <= t <= 2:
                for xi in COLUMNS[u]:
                    for d in both:
                        self.wait("bz", d, xi, t)
                        self.send("bz", d, xi, t + 1)
                if u == 1:
                    self.send_far(t + 1)

    def send_far(self, t):
        if self.far:
            for delta in GROUPS[t]:
                for d in (0, 1):
                    self.send("cx", d, delta)

    def wait_far(self, t):
        for delta in GROUPS[t]:
            for d in (0, 1):
                self.wait("cx", d, delta)

    def settle_a(self, t):
        for delta in GROUPS[t]:
            for d in (0, 1):
                self.wait("ax", d, delta, 1)

    def settle_b(self, u):
        for xi in COLUMNS[u]:
            for d in (0, 1):
                self.wait("bz", d, xi, 3)
        if u == 1:
            self.send_far(4)

    def finish(self):
        for key, piece in self.started:
            z, x, half = self.place(key, 0)
            self.copy(key, z, x, half, piece).wait_send()


def kernel(t_hbm, b_ref, occ_ref, vir_ref, vrow_ref, r_hbm,
           r_v, tf0, tf1, tf2, cd, u, s, bg, acc, fpart, fown, frecv, bvt, labels,
           fg, wf, bvf, rsend, rrecv,
           g_sems, t_send, t_recv, f_send, f_recv,
           w_send, w_recv, v_send, v_recv, r_sem, rr_sem, one):
    z, x, y, v = position()
    o = (z * NX + x) * NY + y
    load_t = pltpu.make_async_copy(t_hbm, r_v, one.at[0])
    load_t.start()
    here = (z * NX + x) * 16
    own = pl.ds(pl.multiple_of(y * 512 + here, 16), 16)

    def place_b(n, _):
        four = jnp.concatenate([b_ref[4 * n + m].astype(F32) for m in range(4)], axis=1)
        bg[own, pl.ds(pl.multiple_of(n * 384, 384), 384)] = four.astype(BF16)
        return 0

    lax.fori_loop(0, 16, place_b, 0)
    barrier(peers_of(z, x, y, v))

    def swap_copy(there):
        rows = pl.ds(pl.multiple_of(there * 512 + here, 16), 16)
        return pltpu.make_async_remote_copy(
            src_ref=bg.at[rows, :], dst_ref=bg.at[rows, :], send_sem=one.at[2], recv_sem=one.at[3],
            device_id=device(z, x, 1 - y, v), device_id_type=MESH)

    def region(kind, half, piece):
        low, middle, high = (0, 1920, 3712) if kind == "a" else (3712, 4992, 6144)
        low, high = (low, high) if half is None else ((low, middle), (middle, high))[half]
        return (0, 16), pl.ds(low, high - low)

    swap_copy(y).start()
    near = Gather(bg, y * 512, 16, region, "", False, g_sems.at[0], g_sems.at[1])
    other = Gather(bg, (1 - y) * 512, 16, region, "", False, g_sems.at[2], g_sems.at[3])
    near.own(0)

    mine_label = occ_ref[o]
    vrow = vrow_ref[...].reshape(1, 384)

    def label_row(k, _):
        labels[pl.ds(k, 1), :] = vrow ^ (occ_ref[k] ^ mine_label)
        return 0

    lax.fori_loop(0, 64, label_row, 0)
    load_t.wait()

    def mask_row(c, _):
        row = r_v[pl.ds(pl.multiple_of(c * 64, 64), 64), :].astype(F32)
        row = jnp.where(labels[...] == vir_ref[v * 96 + c], row, 0.0)
        for n, tf in enumerate((tf0, tf1, tf2)):
            tf[pl.ds(pl.multiple_of(c * 64, 64), 64), :] = row[:, 128 * n:128 * n + 128]
        return 0

    lax.fori_loop(0, 96, mask_row, 0, unroll=4)
    lane = lax.broadcasted_iota(jnp.int32, (96, 128), 1)

    def turn(g, _):
        k = g * 4
        rows = [[tf[pl.ds(k + m, 96, stride=64), :] for tf in (tf0, tf1, tf2)] for m in range(4)]
        for n in range(3):
            for m in range(3):
                packed = jnp.concatenate([rows[m][n], rows[3][n][32 * m:32 * m + 32]], axis=0)
                u[g, m, pl.ds(128 * n, 128), :] = packed.T.astype(BF16)
        for m in range(4):
            a, b, c = rows[m]
            into = pl.ds(pl.multiple_of((k + m) * 96, 96), 96)
            cd[into, pl.ds(0, 128)] = a.astype(BF16)
            cd[into, pl.ds(128, 128)] = jnp.where(
                lane < 32, pltpu.roll(a, 32, 1), pltpu.roll(b, 32, 1)).astype(BF16)
            cd[into, pl.ds(256, 128)] = jnp.where(
                lane < 64, pltpu.roll(b, 64, 1), pltpu.roll(c, 64, 1)).astype(BF16)
            cd[into, pl.ds(384, 128)] = pltpu.roll(c, 96, 1).astype(BF16)
        return 0

    def t_copy(d, sb, wait=False):
        other = (v + NV - d) % NV if wait else (v + d) % NV
        here = other if wait else v
        return pltpu.make_async_remote_copy(
            src_ref=u.at[pl.ds(4 * sb, 4), :, pl.ds(pl.multiple_of(other * 96, 96), 96), :],
            dst_ref=s.at[pl.ds(4 * sb, 4), pl.ds(0, 3), :, pl.ds(pl.multiple_of(here * 128, 128), 128)],
            send_sem=t_send.at[d - 1, sb], recv_sem=t_recv.at[d - 1, sb],
            device_id=device(z, x, y, other), device_id_type=MESH)

    def hand_over(sb):
        lax.fori_loop(4 * sb, 4 * sb + 4, turn, 0)
        for d in range(1, NV):
            t_copy(d, sb).start()

    mine = pltpu.make_async_copy(
        u.at[:, :, pl.ds(pl.multiple_of(v * 96, 96), 96), :],
        s.at[:, pl.ds(0, 3), :, pl.ds(pl.multiple_of(v * 128, 128), 128)], one.at[0])
    def plane(which):
        return pl.ds(pl.multiple_of(512 * (y if which == 0 else 1 - y), 512), 512)

    def combine_group(g, _):
        for blk in range(NV):
            lanes = pl.ds(128 * blk, 128)
            got = [s[g, m, :, lanes].astype(F32) for m in range(3)]
            last = jnp.where(lane < 32, pltpu.roll(got[0], 32, 1), jnp.where(
                lane < 64, pltpu.roll(got[1], 64, 1), pltpu.roll(got[2], 96, 1)))
            for m, other in enumerate(got + [last]):
                straight = cd[pl.ds(pl.multiple_of((4 * g + m) * 96, 96), 96), lanes].astype(F32)
                s[g, m, :, lanes] = (2.0 * straight - other).astype(BF16)
        return 0

    def combine(sb):
        for d in range(1, NV):
            t_copy(d, sb, True).wait_recv()
        lax.fori_loop(4 * sb, 4 * sb + 4, combine_group, 0)

    mate, across = v + 1 - 2 * (v % 2), (v + 2) % NV
    far = (mate + 2) % NV
    two = pl.ds(pl.multiple_of((o % 4 - y) * 96, 96), 192)

    def share_v(step, which, blk):
        rows, lanes = pl.ds(pl.multiple_of(blk * 192, 192), 192), plane(which)
        into = bvf.at[rows, lanes]
        return pltpu.make_async_remote_copy(
            src_ref=into if step == 2 else bvt.at[two, lanes], dst_ref=into,
            send_sem=v_send.at[step, which], recv_sem=v_recv.at[step, which],
            device_id=device(z, x, y, across if step == 1 else mate), device_id_type=MESH)

    def pick(which):
        four = bg[plane(which), pl.ds(pl.multiple_of((o // 4) * 384, 384), 384)]
        bvt[:, plane(which)] = four.astype(F32).T.astype(BF16)

    def f_copy(d, which, wait):
        lanes = plane(which)
        peer = (v + NV - d) % NV if wait else (v + d) % NV
        source = peer if wait else v
        return pltpu.make_async_remote_copy(
            src_ref=fpart.at[peer, :, lanes], dst_ref=frecv.at[source, :, lanes],
            send_sem=f_send.at[d - 1, which], recv_sem=f_recv.at[d - 1, which],
            device_id=device(z, x, y, peer), device_id_type=MESH)

    def fit(parts, low, high, fresh=False):
        def step(kb, _):
            lanes = pl.ds(pl.multiple_of(kb * 768, 768), 768)
            left = [bg[pl.ds(pl.multiple_of(a, 64), size), lanes] for a, size in parts]
            left = left[0] if len(left) == 1 else jnp.concatenate(left, axis=0)
            part = jnp.dot(left, s[pl.ds(kb * 2, 2)].reshape(768, 512), preferred_element_type=F32)
            at = 0
            for a, size in parts:
                into = acc.at[pl.ds(pl.multiple_of(a, 64), size), :]
                piece = part[at:at + size]
                into[...] = (jnp.where(kb == low, 0.0, into[...]) if fresh else into[...]) + piece
                at += size
            return 0

        lax.fori_loop(low, high, step, 0)

    def strips(deltas):
        return [((1 - y) * 512 + (z + delta) % NZ * 64, 64) for delta in deltas]

    whole = [(y * 512, 512)]

    def reduce(which):
        for m in range(4):
            rows = pl.ds(pl.multiple_of(512 * (y if which == 0 else 1 - y) + 128 * m, 128), 128)
            turned = acc[rows, :].T
            for blk in range(NV):
                part = turned[128 * blk:128 * blk + 96]
                fpart[blk, :, rows] = part.astype(BF16)
                fown[blk, :, rows] = part
        for d in range(1, NV):
            f_copy(d, which, False).start()

    block = pl.multiple_of((z * NX + x) * 128, 128)

    def collect(which):
        for d in range(1, NV):
            f_copy(d, which, True).wait_recv()
        lanes = plane(which)
        total = fown[v, :, lanes]
        for d in range(1, NV):
            total = total + frecv[(v + NV - d) % NV, :, lanes].astype(F32)
        total = total.astype(BF16)
        fg[pl.ds(block, 96), lanes] = total
        wf[pl.ds(pl.multiple_of(v * 96, 96), 96), lanes] = total

    def e_copy(which, wait):
        into = plane(1 - which)
        return pltpu.make_async_remote_copy(
            src_ref=fg.at[pl.ds(block + 64, 32), plane(which)], dst_ref=fg.at[pl.ds(block + 96, 32), plane(which) if wait else into],
            send_sem=one.at[4 + which], recv_sem=one.at[6 + which],
            device_id=device(z, x, 1 - y, v), device_id_type=MESH)

    def region2(which):
        def region(kind, half, piece):
            if kind == "b":
                rows = (0, 64) if half is None else (32 * half, 32)
            elif piece is not None:
                rows = (64 + 32 * piece, 32)
            else:
                rows = (64, 64) if half is None else (64 + 32 * half, 32)
            return rows, plane(which)

        return region

    first_half = Gather(fg, 0, 128, region2(0), "a", True, g_sems.at[4], g_sems.at[5])
    second_half = Gather(fg, 0, 128, region2(1), "a", True, g_sems.at[6], g_sems.at[7])

    hand_over(0)
    near.wave(1)
    hand_over(1)
    near.wave(2)
    hand_over(2)
    hand_over(3)
    mine.start()
    near.wave(3)
    swap_copy(1 - y).wait_recv()
    other.own(0)
    near.wave(4)
    near.wave(5)
    for n in range(3):
        near.settle_b(n)
    for n in range(5):
        near.settle_a(n)
    pick(0)
    share_v(1, 0, v).start()
    share_v(0, 0, v).start()
    other.wave(1)
    mine.wait()
    combine(0)
    combine(1)
    other.wave(2)
    fit(whole, 0, 4, True)
    other.wave(3)
    combine(2)
    fit(whole, 4, 6)
    other.wave(4)
    combine(3)
    fit(whole, 6, 8)
    reduce(0)
    other.wave(5)
    for n in range(2):
        other.settle_a(n)
    fit(strips((0, 1, 7)), 0, 8, True)
    collect(0)
    e_copy(0, False).start()
    first_half.own(0)
    other.settle_a(2)
    fit(strips((2, 6)), 0, 8, True)
    share_v(1, 0, across).wait_recv()
    share_v(2, 0, across).start()
    e_copy(0, True).wait_recv()
    first_half.own(1)
    for n in range(3):
        other.settle_b(n)
    fit(strips((3, 5, 4)), 5, 8, True)
    first_half.wave(1)
    for n in range(3, 5):
        other.settle_a(n)
    fit(strips((3, 5, 4)), 0, 5)
    reduce(1)
    pick(1)
    same = pltpu.make_async_copy(bvt.at[two, :], bvf.at[pl.ds(pl.multiple_of(v * 192, 192), 192), :], one.at[0])
    same.start()
    first_half.wave(2)
    collect(1)
    e_copy(1, False).start()
    second_half.own(0)
    share_v(1, 1, v).start()
    share_v(0, 1, v).start()

    def share_w(step, blk):
        rows = pl.ds(pl.multiple_of(blk * 96, 96), 96)
        return pltpu.make_async_remote_copy(
            src_ref=wf.at[rows, :], dst_ref=wf.at[rows, :], send_sem=w_send.at[step], recv_sem=w_recv.at[step],
            device_id=device(z, x, y, across if step == 1 else mate), device_id_type=MESH)

    share_w(1, v).start()
    share_w(0, v).start()
    first_half.wave(3)
    e_copy(1, True).wait_recv()
    second_half.own(1)
    share_v(1, 1, across).wait_recv()
    share_v(2, 1, across).start()
    second_half.wave(1)
    share_w(1, across).wait_recv()
    share_w(2, across).start()
    same.wait()
    for which in range(2):
        share_v(0, which, mate).wait_recv()
        share_v(2, which, far).wait_recv()
    first, second, third, turned = (cd.at[pl.ds(1024 * n, 1024), pl.ds(0, 384)] for n in range(4))
    for ref, which in ((second, 1 - y), (first, y)):
        wide = jnp.concatenate(
            [bvf[pl.ds(pl.multiple_of(blk * 192 + which * 96, 96), 96), :] for blk in range(NV)], axis=0)
        ref[...] = wide.astype(F32).T.astype(BF16)
    turned[pl.ds(0, 512), :] = first[pl.ds(512, 512), :]
    turned[pl.ds(512, 512), :] = first[pl.ds(0, 512), :]

    def direct(n, _):
        lanes = pl.ds(pl.multiple_of(n * 384, 384), 384)
        part = lax.dot_general(bg[:, lanes], third[...], (((0,), (0,)), ((), ())), preferred_element_type=F32)
        r_v[pl.ds(pl.multiple_of(n * 384, 384), 384), :] = part.astype(BF16)
        return 0

    def add(row, size, part):
        rows = pl.ds(pl.multiple_of(row, 32), size)
        r_v[rows, :] = (r_v[rows, :].astype(F32) + part).astype(BF16)

    def spot(delta, xi):
        return (z + delta) % NZ * NX + (x + xi) % NX

    def r_copy(delta, xi):
        rows = pl.ds(pl.multiple_of(spot(delta, xi) * 64, 64), 64)
        return pltpu.make_async_remote_copy(
            src_ref=rsend.at[rows, :], dst_ref=rrecv.at[rows, :], send_sem=r_sem.at[delta * NX + xi],
            recv_sem=rr_sem.at[delta * NX + xi], device_id=device(z, x, 1 - y, v), device_id_type=MESH)

    def front(w):
        return [(delta, xi) for u in range(3) for xi in COLUMNS[u] if 0 <= w - u <= 4 for delta in GROUPS[w - u]]

    def early_rows(w):
        return jnp.concatenate(
            [fg[pl.ds(pl.multiple_of(spot(*at) * 128, 128), 64), :] for at in front(w)], axis=0)

    def theirs(w):
        part = jnp.dot(early_rows(w), second[...], preferred_element_type=F32).astype(BF16)
        for n, at in enumerate(front(w)):
            rsend[pl.ds(pl.multiple_of(spot(*at) * 64, 64), 64), :] = part[64 * n:64 * n + 64]
            r_copy(*at).start()

    def ours_early(w):
        part = jnp.dot(early_rows(w), first[...], preferred_element_type=F32)
        for n, at in enumerate(front(w)):
            add((spot(*at) * NY + y) * 96, 64, part[64 * n:64 * n + 64])

    def ours_late(t):
        for delta in GROUPS[t]:
            for start, weights, row in ((64, first, y * 96 + 64), (96, turned, (1 - y) * 96 + 64)):
                left = jnp.concatenate(
                    [fg[pl.ds(pl.multiple_of(spot(delta, m) * 128 + start, 32), 32), :] for m in range(NX)], axis=0)
                part = jnp.dot(left, weights[...], preferred_element_type=F32)
                for m in range(NX):
                    add(spot(delta, m) * NY * 96 + row, 32, part[32 * m:32 * m + 32])

    def arrived(w):
        for at in front(w):
            r_copy(*at).wait_recv()
            got = rrecv[pl.ds(pl.multiple_of(spot(*at) * 64, 64), 64), :].astype(F32)
            add((spot(*at) * NY + 1 - y) * 96, 64, got)

    theirs(0)
    theirs(1)
    first_half.wave(4)
    first_half.settle_b(0)
    second_half.wave(2)
    theirs(2)
    share_w(0, mate).wait_recv()
    share_w(2, far).wait_recv()
    third[...] = wf[...].astype(F32).T.astype(BF16)
    first_half.wave(5)
    first_half.settle_b(1)
    lax.fori_loop(0, 8, direct, 0)
    second_half.wave(3)
    first_half.wait_far(1)
    second_half.wait_far(1)
    theirs(3)
    lax.fori_loop(8, 16, direct, 0)
    for w in range(4):
        ours_early(w)
    second_half.wave(4)
    second_half.settle_b(0)
    first_half.wait_far(2)
    second_half.wait_far(2)
    theirs(4)
    ours_early(4)
    first_half.settle_b(2)
    first_half.wait_far(3)
    first_half.wait_far(4)
    for t in range(5):
        first_half.settle_a(t)
    for t in range(2):
        second_half.settle_a(t)
        ours_late(t)
    for w in range(3):
        arrived(w)
    second_half.wave(5)
    second_half.settle_b(1)
    second_half.wait_far(3)
    theirs(5)
    ours_early(5)
    second_half.settle_a(2)
    ours_late(2)
    arrived(3)
    second_half.settle_b(2)
    second_half.wait_far(4)
    theirs(6)
    ours_early(6)
    second_half.settle_a(3)
    ours_late(3)
    arrived(4)
    second_half.settle_a(4)
    ours_late(4)
    arrived(5)
    arrived(6)
    save = pltpu.make_async_copy(r_v, r_hbm, one.at[0])
    save.start()

    for d in range(1, NV):
        for which in range(2):
            f_copy(d, which, False).wait_send()
        for sb in range(4):
            t_copy(d, sb).wait_send()
    swap_copy(y).wait_send()
    for step in range(3):
        share_w(step, across if step == 2 else v).wait_send()
        for which in range(2):
            share_v(step, which, across if step == 2 else v).wait_send()
    for which in range(2):
        e_copy(which, False).wait_send()
    for delta in range(NZ):
        for xi in range(NX):
            r_copy(delta, xi).wait_send()
    for ring in (near, other, first_half, second_half):
        ring.finish()
    save.wait()


def on_device(amplitudes, aux_ints, occ_irrep, vir_irrep):
    any_spec = pl.BlockSpec(memory_space=pl.ANY)
    vmem_spec = pl.BlockSpec(memory_space=pltpu.VMEM)
    smem_spec = pl.BlockSpec(memory_space=pltpu.SMEM)
    dma, vmem = pltpu.SemaphoreType.DMA, pltpu.VMEM
    r = pl.pallas_call(
        kernel,
        name="ccsd",
        out_shape=jax.ShapeDtypeStruct((6144, 384), BF16),
        in_specs=[any_spec, vmem_spec, smem_spec, smem_spec, vmem_spec],
        out_specs=any_spec,
        scratch_shapes=[
            vmem((6144, 384), BF16), vmem((6144, 128), F32), vmem((6144, 128), F32), vmem((6144, 128), F32),
            vmem((6144, 512), BF16), vmem((16, 3, 384, 128), BF16), vmem((16, 4, 96, 512), BF16),
            vmem((1024, 6144), BF16), vmem((1024, 512), F32), vmem((NV, 96, 1024), BF16),
            vmem((NV, 96, 1024), F32), vmem((NV, 96, 1024), BF16), vmem((384, 1024), BF16),
            vmem((64, 384), jnp.int32),
            vmem((4096, 1024), BF16), vmem((384, 1024), BF16), vmem((768, 1024), BF16),
            vmem((2048, 384), BF16), vmem((2048, 384), BF16),
            dma((8, N_SEMS)),
            dma((3, 4)), dma((3, 4)), dma((3, 2)), dma((3, 2)),
            dma((3,)), dma((3,)), dma((3, 2)), dma((3, 2)), dma((32,)), dma((32,)), dma((8,)),
        ],
        compiler_params=pltpu.CompilerParams(collective_id=0, has_side_effects=True, vmem_limit_bytes=63 << 20),
    )(amplitudes.reshape(6144, 384), jnp.transpose(aux_ints, (1, 2, 0)), occ_irrep, vir_irrep, vir_irrep)
    return jnp.transpose(r.reshape(64, 96, 384), (1, 0, 2))[None]


def solution(mesh):
    in_specs = (P("occ", "vir", None, None), P("vir", None, "occ"), P(), P())
    out_specs = P("occ", "vir", None, None)
    return jax.shard_map(
        on_device, mesh=mesh, in_specs=in_specs, out_specs=out_specs, check_vma=False
    )
```

```python
import functools

import jax
import jax.numpy as jnp
from jax import lax
from jax.experimental import pallas as pl
from jax.experimental.pallas import tpu as pltpu
from jax.sharding import PartitionSpec as P

MESH = pl.DeviceIdType.MESH
NZ, NX, NY, NV = 8, 4, 2, 4
BF16, F32 = jnp.bfloat16, jnp.float32
GROUPS = ((0,), (1, 7), (2, 6), (3, 5), (4,))
COLUMNS = ((0,), (1, 3), (2,))
N_SEMS = 100


def position():
    o, v = lax.axis_index("occ"), lax.axis_index("vir")
    return o >> 3, (o >> 1) & (NX - 1), o & (NY - 1), v


def device(z, x, y, v):
    return ((z * NX + x) * NY + y, v)


def barrier(peers):
    sem = pltpu.get_barrier_semaphore()
    for peer in peers:
        pl.semaphore_signal(sem, 1, device_id=peer, device_id_type=MESH)
    pl.semaphore_wait(sem, len(peers))


def peers_of(z, x, y, v):
    ring = [
        device((z + 1) % NZ, x, y, v),
        device((z + NZ - 1) % NZ, x, y, v),
        device(z, (x + 1) % NX, y, v),
        device(z, (x + NX - 1) % NX, y, v),
        device(z, x, 1 - y, v),
    ]
    return ring + [device(z, x, y, (v + d) & (NV - 1)) for d in range(1, NV)]


class Gather:
    def __init__(self, ref, block, region, two_pieces, far, send_sems, recv_sems):
        self.ref, self.block, self.region, self.two_pieces, self.far = ref, block, region, two_pieces, far
        self.send_sems, self.recv_sems = send_sems, recv_sems
        z, x, y, v = position()
        self.z_rows = [((z + n) & (NZ - 1)) * (NX * block) for n in range(NZ)]
        self.x_rows = [((x + n) & (NX - 1)) * block for n in range(NX)]
        self.targets = {
            "z": [device((z + n) & (NZ - 1), x, y, v) for n in (1, NZ - 1)],
            "x": [device(z, (x + n) & (NX - 1), y, v) for n in (1, NX - 1)],
        }
        self.started = []

    def copy(self, key, z, x, half, piece):
        kind, d = key[0], key[1]
        if kind == "az":
            index = d * 4 + key[2]
        elif kind == "ax":
            index = 8 + (d * 8 + key[2]) * 2 + key[3]
        elif kind == "bx":
            index = 40 + d * 2 + key[2]
        elif kind == "bz":
            index = 44 + (d * 4 + key[2]) * 4 + key[3]
        else:
            index = 84 + d * 8 + key[2]
        if piece == 1:
            index = 76 + {"az": 0, "ax": 1, "bx": 2, "bz": 3}[kind] * 2 + d
        if kind == "cx":
            (start, size), lanes = (48 - 16 * d, 16), pl.ds(0, self.ref.shape[1])
        elif self.far and kind == "bz" and key[2] == 2:
            (start, size), lanes = (0, 32) if half is None else (16 * half, 16), pl.ds(0, self.ref.shape[1])
        else:
            (start, size), lanes = self.region(kind[0], half, piece)
        rows = pl.ds(pl.multiple_of(self.z_rows[z % NZ] + self.x_rows[x % NX] + start, 16), size)
        part = self.ref.at[rows, lanes]
        target = self.targets[kind[1]][d]
        return pltpu.make_async_remote_copy(
            src_ref=part, dst_ref=part, send_sem=self.send_sems.at[index],
            recv_sem=self.recv_sems.at[index], device_id=target, device_id_type=MESH)

    def place(self, key, behind):
        kind, d = key[0], key[1]
        s = 1 - 2 * d
        half = None
        if kind == "az":
            dz, dx = -s * (key[2] + behind), 0
            half = d if key[2] == 3 else None
        elif kind == "ax":
            dz, dx = key[2], -s * (key[3] + behind)
            half = d if key[3] == 1 else None
        elif kind == "bx":
            dz, dx = 0, -s * (key[2] + behind)
            half = d if key[2] == 1 else None
        elif kind == "bz":
            dz, dx = -s * (key[3] + behind), key[2]
            half = d if key[3] == 3 else None
        else:
            dz, dx = key[2], -s * (1 + behind)
        return dz, dx, half

    def pieces(self, key):
        own = key[0] != "cx" and key[2:] in ((0,), (0, 0))
        if not own:
            return (None,)
        return (0, 1) if key[0][0] in self.two_pieces else (0,)

    def send(self, *key, piece=None):
        z, x, half = self.place(key, 0)
        self.copy(key, z, x, half, piece).start()
        self.started.append((key, piece))

    def wait(self, *key):
        z, x, half = self.place(key, 1)
        for piece in self.pieces(key):
            self.copy(key, z, x, half, piece).wait_recv()

    def own(self, piece):
        for kind in (("az", "bx"), ("ax", "bz")):
            for d in (0, 1):
                for name in kind:
                    key = (name, d, 0) if name in ("az", "bx") else (name, d, 0, 0)
                    if piece in self.pieces(key):
                        self.send(*key, piece=piece)

    def wave(self, w):
        both = (0, 1)
        if w <= 4:
            for d in both:
                self.wait("az", d, w - 1)
                if w <= 3:
                    self.send("az", d, w)
            for delta in GROUPS[w]:
                for d in both:
                    self.send("ax", d, delta, 0)
        if w == 1:
            for d in both:
                self.wait("bx", d, 0)
                self.send("bx", d, 1)
            for xi in COLUMNS[1]:
                for d in both:
                    self.send("bz", d, xi, 0)
        if w == 2:
            for d in both:
                self.wait("bx", d, 1)
            for d in both:
                self.send("bz", d, 2, 0)
        for delta in GROUPS[w - 1]:
            for d in both:
                self.wait("ax", d, delta, 0)
                self.send("ax", d, delta, 1)
        for u in range(3):
            t = w - 1 - u
            if 0 <= t <= 2:
                for xi in COLUMNS[u]:
                    for d in both:
                        self.wait("bz", d, xi, t)
                        self.send("bz", d, xi, t + 1)
                if u == 1:
                    self.send_far(t + 1)

    def send_far(self, t):
        if self.far:
            for delta in GROUPS[t]:
                for d in (0, 1):
                    self.send("cx", d, delta)

    def wait_far(self, t):
        for delta in GROUPS[t]:
            for d in (0, 1):
                self.wait("cx", d, delta)

    def settle_a(self, t):
        for delta in GROUPS[t]:
            for d in (0, 1):
                self.wait("ax", d, delta, 1)

    def settle_b(self, u):
        for xi in COLUMNS[u]:
            for d in (0, 1):
                self.wait("bz", d, xi, 3)
        if u == 1:
            self.send_far(4)

    def finish(self):
        for key, piece in self.started:
            z, x, half = self.place(key, 0)
            self.copy(key, z, x, half, piece).wait_send()


def kernel(t_hbm, b_ref, occ_ref, vir_ref, vrow_ref, r_hbm,
           r_v, tf0, tf1, tf2, cd, u, s, bg, acc, fpart, fown, frecv, bvt, labels,
           fg, wf, bvf, rsend, rrecv,
           g_send, g_recv, g2_send, g2_recv, t_send, t_recv, f_send, f_recv,
           w_send, w_recv, v_send, v_recv, r_sem, rr_sem, out_sem, one):
    z, x, y, v = position()
    o = (z * NX + x) * NY + y
    load_t = pltpu.make_async_copy(t_hbm, r_v, one.at[0])
    load_t.start()
    own = pl.ds(pl.multiple_of(o * 16, 16), 16)

    def place_b(n, _):
        four = jnp.concatenate([b_ref[4 * n + m].astype(F32) for m in range(4)], axis=1)
        bg[own, pl.ds(pl.multiple_of(n * 384, 384), 384)] = four.astype(BF16)
        return 0

    lax.fori_loop(0, 16, place_b, 0)
    barrier(peers_of(z, x, y, v))

    def swap_copy(there):
        rows = pl.ds(pl.multiple_of((o - y + there) * 16, 16), 16)
        return pltpu.make_async_remote_copy(
            src_ref=bg.at[rows, :], dst_ref=bg.at[rows, :], send_sem=one.at[2], recv_sem=one.at[3],
            device_id=device(z, x, 1 - y, v), device_id_type=MESH)

    def region(kind, half, piece):
        if piece is not None:
            rows = ((y if piece == 0 else 1 - y) * 16, 16)
        elif half is not None:
            rows = (half * 16, 16)
        else:
            rows = (0, 32)
        return rows, pl.ds(0, 3712) if kind == "a" else pl.ds(3712, 6144 - 3712)

    swap_copy(y).start()
    gather = Gather(bg, 32, region, "ab", False, g_send, g_recv)
    gather.own(0)

    mine_label = occ_ref[o]
    vrow = vrow_ref[...].reshape(1, 384)

    def label_row(k, _):
        labels[pl.ds(k, 1), :] = vrow ^ (occ_ref[k] ^ mine_label)
        return 0

    lax.fori_loop(0, 64, label_row, 0)
    load_t.wait()

    def mask(sb):
        wanted = labels[pl.ds(16 * sb, 16), :]

        def mask_row(c, _):
            rows = pl.ds(pl.multiple_of(c * 64 + 16 * sb, 16), 16)
            row = jnp.where(wanted == vir_ref[v * 96 + c], r_v[rows, :].astype(F32), 0.0)
            for n, tf in enumerate((tf0, tf1, tf2)):
                tf[rows, :] = row[:, 128 * n:128 * n + 128]
            return 0

        lax.fori_loop(0, 96, mask_row, 0, unroll=8)


    lane = lax.broadcasted_iota(jnp.int32, (96, 128), 1)

    def turn(g, _):
        k = g * 4
        rows = [[tf[pl.ds(k + m, 96, stride=64), :] for tf in (tf0, tf1, tf2)] for m in range(4)]
        for n in range(3):
            for m in range(3):
                packed = jnp.concatenate([rows[m][n], rows[3][n][32 * m:32 * m + 32]], axis=0)
                u[g, m, pl.ds(128 * n, 128), :] = packed.T.astype(BF16)
        for m in range(4):
            a, b, c = rows[m]
            into = pl.ds(pl.multiple_of((k + m) * 96, 96), 96)
            cd[into, pl.ds(0, 128)] = a.astype(BF16)
            cd[into, pl.ds(128, 128)] = jnp.where(
                lane < 32, pltpu.roll(a, 32, 1), pltpu.roll(b, 32, 1)).astype(BF16)
            cd[into, pl.ds(256, 128)] = jnp.where(
                lane < 64, pltpu.roll(b, 64, 1), pltpu.roll(c, 64, 1)).astype(BF16)
            cd[into, pl.ds(384, 128)] = pltpu.roll(c, 96, 1).astype(BF16)
        return 0

    def t_copy(d, sb, wait=False):
        other = (v + NV - d) & (NV - 1) if wait else (v + d) & (NV - 1)
        here = other if wait else v
        return pltpu.make_async_remote_copy(
            src_ref=u.at[pl.ds(4 * sb, 4), :, pl.ds(pl.multiple_of(other * 96, 96), 96), :],
            dst_ref=s.at[pl.ds(4 * sb, 4), pl.ds(0, 3), :, pl.ds(pl.multiple_of(here * 128, 128), 128)],
            send_sem=t_send.at[d - 1, sb], recv_sem=t_recv.at[d - 1, sb],
            device_id=device(z, x, y, other), device_id_type=MESH)

    def hand_over(sb):
        mask(sb)
        lax.fori_loop(4 * sb, 4 * sb + 4, turn, 0)
        for d in range(1, NV):
            t_copy(d, sb).start()

    mine = pltpu.make_async_copy(
        u.at[:, :, pl.ds(pl.multiple_of(v * 96, 96), 96), :],
        s.at[:, pl.ds(0, 3), :, pl.ds(pl.multiple_of(v * 128, 128), 128)], one.at[0])
    pairs = ((0, 1), (7, 2), (6, 3), (5, 4))

    def zrow(delta):
        return pl.multiple_of((((z + delta) & (NZ - 1))) * 128, 128)

    def combine_group(g, _):
        for blk in range(NV):
            lanes = pl.ds(128 * blk, 128)
            got = [s[g, m, :, lanes].astype(F32) for m in range(3)]
            last = jnp.where(lane < 32, pltpu.roll(got[0], 32, 1), jnp.where(
                lane < 64, pltpu.roll(got[1], 64, 1), pltpu.roll(got[2], 96, 1)))
            for m, other in enumerate(got + [last]):
                straight = cd[pl.ds(pl.multiple_of((4 * g + m) * 96, 96), 96), lanes].astype(F32)
                s[g, m, :, lanes] = (2.0 * straight - other).astype(BF16)
        return 0

    def combine(sb):
        for d in range(1, NV):
            t_copy(d, sb, True).wait_recv()
        lax.fori_loop(4 * sb, 4 * sb + 4, combine_group, 0)

    mate, across = v + 1 - 2 * (v % 2), (v + 2) & (NV - 1)
    far = (mate + 2) & (NV - 1)
    two = pl.ds(pl.multiple_of((o % 4 - y) * 96, 96), 192)

    def share_v(step, delta, blk):
        rows, lanes = pl.ds(pl.multiple_of(blk * 192, 192), 192), pl.ds(zrow(delta), 128)
        into = bvf.at[rows, lanes]
        return pltpu.make_async_remote_copy(
            src_ref=into if step == 2 else bvt.at[two, lanes], dst_ref=into,
            send_sem=v_send.at[step, delta], recv_sem=v_recv.at[step, delta],
            device_id=device(z, x, y, across if step == 1 else mate), device_id_type=MESH)

    def pick(n):
        for delta in pairs[n]:
            rows = pl.ds(zrow(delta), 128)
            four = bg[rows, pl.ds(pl.multiple_of((o // 4) * 384, 384), 384)]
            bvt[:, rows] = four.astype(F32).T.astype(BF16)

    def f_copy(d, delta, wait):
        lanes = pl.ds(zrow(delta), 128)
        other = (v + NV - d) & (NV - 1) if wait else (v + d) & (NV - 1)
        here = other if wait else v
        return pltpu.make_async_remote_copy(
            src_ref=fpart.at[other, :, lanes], dst_ref=frecv.at[here, :, lanes],
            send_sem=f_send.at[d - 1, delta], recv_sem=f_recv.at[d - 1, delta],
            device_id=device(z, x, y, other), device_id_type=MESH)

    def fit(n, low, high, fresh=False):
        starts = [zrow(delta) for delta in pairs[n]]
        total = acc.at[pl.ds(256 * n, 256), :]

        def step(kb, _):
            lanes = pl.ds(pl.multiple_of(kb * 768, 768), 768)
            left = jnp.concatenate([bg[pl.ds(a, 128), lanes] for a in starts], axis=0)
            part = jnp.dot(left, s[pl.ds(kb * 2, 2)].reshape(768, 512), preferred_element_type=F32)
            total[...] = (jnp.where(kb == low, 0.0, total[...]) if fresh else total[...]) + part
            return 0

        lax.fori_loop(low, high, step, 0)

    def reduce(n):
        for m, delta in enumerate(pairs[n]):
            rows = pl.ds(zrow(delta), 128)
            turned = acc[pl.ds(256 * n + 128 * m, 128), :].T
            for blk in range(NV):
                part = turned[128 * blk:128 * blk + 96]
                fpart[blk, :, rows] = part.astype(BF16)
                fown[blk, :, rows] = part
            for d in range(1, NV):
                f_copy(d, delta, False).start()

    hand_over(0)
    swap_copy(1 - y).wait_recv()
    gather.own(1)
    gather.wave(1)
    hand_over(1)
    gather.wave(2)
    hand_over(2)
    hand_over(3)
    mine.start()
    gather.wave(3)
    gather.settle_a(0)
    gather.settle_a(1)
    pick(0)
    mine.wait()
    combine(0)
    combine(1)
    fit(0, 0, 4, True)
    gather.wave(4)
    gather.settle_a(2)
    pick(1)
    for n in range(2):
        for delta in pairs[n]:
            share_v(1, delta, v).start()
            share_v(0, delta, v).start()
    combine(2)
    fit(0, 4, 6)
    fit(1, 0, 6, True)
    gather.wave(5)
    combine(3)
    fit(0, 6, 8)
    reduce(0)
    fit(1, 6, 8)
    reduce(1)
    fit(2, 5, 8, True)
    gather.settle_a(3)
    fit(2, 0, 5)
    reduce(2)
    for column in range(3):
        gather.settle_b(column)
    fit(3, 5, 8, True)
    gather.settle_a(4)
    fit(3, 0, 5)
    reduce(3)
    pick(2)
    pick(3)
    for n in range(2):
        for delta in pairs[n]:
            share_v(1, delta, across).wait_recv()
            share_v(2, delta, across).start()
    same = pltpu.make_async_copy(bvt.at[two, :], bvf.at[pl.ds(pl.multiple_of(v * 192, 192), 192), :], one.at[0])
    same.start()

    for d in range(1, NV):
        for delta in range(NZ):
            f_copy(d, delta, True).wait_recv()
    total = fown[v]
    for d in range(1, NV):
        total = total + frecv[(v + NV - d) & (NV - 1)].astype(F32)
    total = total.astype(BF16)
    block = pl.multiple_of((z * NX + x) * 128, 128)
    fg[pl.ds(block, 96), :] = total
    wf[pl.ds(pl.multiple_of(v * 96, 96), 96), :] = total

    swap = pltpu.make_async_remote_copy(
        src_ref=fg.at[pl.ds(block + 64, 32), :], dst_ref=fg.at[pl.ds(block + 96, 32), :],
        send_sem=one.at[4], recv_sem=one.at[5], device_id=device(z, x, 1 - y, v), device_id_type=MESH)
    swap.start()

    def share_w(step, blk):
        rows = pl.ds(pl.multiple_of(blk * 96, 96), 96)
        return pltpu.make_async_remote_copy(
            src_ref=wf.at[rows, :], dst_ref=wf.at[rows, :], send_sem=w_send.at[step], recv_sem=w_recv.at[step],
            device_id=device(z, x, y, across if step == 1 else mate), device_id_type=MESH)

    def region2(kind, half, piece):
        if kind == "b":
            rows = (0, 64) if half is None else (32 * half, 32)
        elif piece is not None:
            rows = (64 + 32 * piece, 32)
        else:
            rows = (64, 64) if half is None else (64 + 32 * half, 32)
        return rows, pl.ds(0, 1024)

    again = Gather(fg, 128, region2, "a", True, g2_send, g2_recv)
    again.own(0)
    same.wait()
    late = pairs[2] + pairs[3]
    for delta in late:
        share_v(1, delta, v).start()
        share_v(0, delta, v).start()
    share_w(1, v).start()
    share_w(0, v).start()
    swap.wait_recv()
    again.own(1)
    for delta in late:
        share_v(1, delta, across).wait_recv()
        share_v(2, delta, across).start()
    again.wave(1)
    share_w(1, across).wait_recv()
    share_w(2, across).start()
    for delta in range(NZ):
        share_v(0, delta, mate).wait_recv()
        share_v(2, delta, far).wait_recv()
    first, second, third = (cd.at[pl.ds(1024 * n, 1024), pl.ds(0, 384)] for n in range(3))
    for ref, which in ((second, 1 - y), (first, y)):
        whole = jnp.concatenate(
            [bvf[pl.ds(pl.multiple_of(blk * 192 + which * 96, 96), 96), :] for blk in range(NV)], axis=0)
        ref[...] = whole.astype(F32).T.astype(BF16)

    def direct(n, _):
        lanes = pl.ds(pl.multiple_of(n * 384, 384), 384)
        part = lax.dot_general(bg[:, lanes], third[...], (((0,), (0,)), ((), ())), preferred_element_type=F32)
        r_v[pl.ds(pl.multiple_of(n * 384, 384), 384), :] = part.astype(BF16)
        return 0

    def add(row, size, part):
        rows = pl.ds(pl.multiple_of(row, 32), size)
        r_v[rows, :] = (r_v[rows, :].astype(F32) + part).astype(BF16)

    def spot(delta, xi):
        return ((z + delta) & (NZ - 1)) * NX + ((x + xi) & (NX - 1))

    def r_copy(delta, xi):
        rows = pl.ds(pl.multiple_of(spot(delta, xi) * 64, 64), 64)
        return pltpu.make_async_remote_copy(
            src_ref=rsend.at[rows, :], dst_ref=rrecv.at[rows, :], send_sem=r_sem.at[delta * NX + xi],
            recv_sem=rr_sem.at[delta * NX + xi], device_id=device(z, x, 1 - y, v), device_id_type=MESH)

    def front(w):
        return [(delta, xi) for u in range(3) for xi in COLUMNS[u] if 0 <= w - u <= 4 for delta in GROUPS[w - u]]

    def early_rows(w):
        return jnp.concatenate(
            [fg[pl.ds(pl.multiple_of(spot(*at) * 128, 128), 64), :] for at in front(w)], axis=0)

    def theirs(w):
        part = jnp.dot(early_rows(w), second[...], preferred_element_type=F32).astype(BF16)
        for n, at in enumerate(front(w)):
            rsend[pl.ds(pl.multiple_of(spot(*at) * 64, 64), 64), :] = part[64 * n:64 * n + 64]
            r_copy(*at).start()

    def ours_early(w):
        part = jnp.dot(early_rows(w), first[...], preferred_element_type=F32)
        for n, at in enumerate(front(w)):
            add((spot(*at) * NY + y) * 96, 64, part[64 * n:64 * n + 64])

    def ours_late(t):
        for delta in GROUPS[t]:
            left = jnp.concatenate(
                [fg[pl.ds(pl.multiple_of(spot(delta, m) * 128 + 64, 64), 64), :] for m in range(NX)], axis=0)
            part = jnp.dot(left, first[...], preferred_element_type=F32)
            for m in range(NX):
                pair = spot(delta, m) * NY
                add((pair + y) * 96 + 64, 32, part[64 * m:64 * m + 32])
                add((pair + 1 - y) * 96 + 64, 32, part[64 * m + 32:64 * m + 64])

    def arrived(w):
        for at in front(w):
            r_copy(*at).wait_recv()
            got = rrecv[pl.ds(pl.multiple_of(spot(*at) * 64, 64), 64), :].astype(F32)
            add((spot(*at) * NY + 1 - y) * 96, 64, got)

    def save_copy(delta):
        rows = pl.ds(pl.multiple_of(((z + delta) & (NZ - 1)) * 768, 768), 768)
        return pltpu.make_async_copy(r_v.at[rows, :], r_hbm.at[rows, :], out_sem.at[delta])

    def save(t):
        for delta in GROUPS[t]:
            save_copy(delta).start()

    theirs(0)
    theirs(1)
    again.wave(2)
    theirs(2)
    share_w(0, mate).wait_recv()
    share_w(2, far).wait_recv()
    third[...] = wf[...].astype(F32).T.astype(BF16)
    lax.fori_loop(0, 8, direct, 0)
    again.wave(3)
    again.wait_far(1)
    theirs(3)
    lax.fori_loop(8, 16, direct, 0)
    for w in range(4):
        ours_early(w)
    again.wave(4)
    again.settle_b(0)
    again.wait_far(2)
    theirs(4)
    ours_early(4)
    for t in range(2):
        again.settle_a(t)
        ours_late(t)
    for w in range(3):
        arrived(w)
    save(0)
    again.wave(5)
    again.settle_b(1)
    again.wait_far(3)
    theirs(5)
    ours_early(5)
    again.settle_a(2)
    ours_late(2)
    arrived(3)
    save(1)
    again.settle_b(2)
    again.wait_far(4)
    theirs(6)
    ours_early(6)
    again.settle_a(3)
    ours_late(3)
    arrived(4)
    save(2)
    again.settle_a(4)
    ours_late(4)
    arrived(5)
    save(3)
    arrived(6)
    save(4)

    for d in range(1, NV):
        for delta in range(NZ):
            f_copy(d, delta, False).wait_send()
        for sb in range(4):
            t_copy(d, sb).wait_send()
    swap_copy(y).wait_send()
    gather.finish()
    swap.wait_send()
    for step in range(3):
        share_w(step, across if step == 2 else v).wait_send()
        for delta in range(NZ):
            share_v(step, delta, across if step == 2 else v).wait_send()
    for delta in range(NZ):
        for xi in range(NX):
            r_copy(delta, xi).wait_send()
    again.finish()
    for delta in range(NZ):
        save_copy(delta).wait()


def on_device(amplitudes, aux_ints, occ_irrep, vir_irrep):
    any_spec = pl.BlockSpec(memory_space=pl.ANY)
    vmem_spec = pl.BlockSpec(memory_space=pltpu.VMEM)
    smem_spec = pl.BlockSpec(memory_space=pltpu.SMEM)
    dma, vmem = pltpu.SemaphoreType.DMA, pltpu.VMEM
    r = pl.pallas_call(
        kernel,
        name="ccsd",
        out_shape=jax.ShapeDtypeStruct((6144, 384), BF16),
        in_specs=[any_spec, vmem_spec, smem_spec, smem_spec, vmem_spec],
        out_specs=any_spec,
        scratch_shapes=[
            vmem((6144, 384), BF16), vmem((6144, 128), F32), vmem((6144, 128), F32), vmem((6144, 128), F32),
            vmem((6144, 512), BF16), vmem((16, 3, 384, 128), BF16), vmem((16, 4, 96, 512), BF16),
            vmem((1024, 6144), BF16), vmem((1024, 512), F32), vmem((NV, 96, 1024), BF16),
            vmem((NV, 96, 1024), F32), vmem((NV, 96, 1024), BF16), vmem((384, 1024), BF16),
            vmem((64, 384), jnp.int32),
            vmem((4096, 1024), BF16), vmem((384, 1024), BF16), vmem((768, 1024), BF16),
            vmem((2048, 384), BF16), vmem((2048, 384), BF16),
            dma((N_SEMS,)), dma((N_SEMS,)), dma((N_SEMS,)), dma((N_SEMS,)),
            dma((3, 4)), dma((3, 4)), dma((3, 8)), dma((3, 8)),
            dma((3,)), dma((3,)), dma((3, 8)), dma((3, 8)), dma((32,)), dma((32,)), dma((8,)), dma((6,)),
        ],
        compiler_params=pltpu.CompilerParams(collective_id=0, has_side_effects=True, vmem_limit_bytes=63 << 20),
    )(amplitudes.reshape(6144, 384), jnp.transpose(aux_ints, (1, 2, 0)), occ_irrep, vir_irrep, vir_irrep)
    return jnp.transpose(r.reshape(64, 96, 384), (1, 0, 2))[None]


def solution(mesh):
    in_specs = (P("occ", "vir", None, None), P("vir", None, "occ"), P(), P())
    out_specs = P("occ", "vir", None, None)
    return jax.shard_map(
        on_device, mesh=mesh, in_specs=in_specs, out_specs=out_specs, check_vma=False
    )
```
